256 devices in a mesh: ctx: 16 (over y_lo, z), ep: 16 (over y_hi, x, core).
Axes of the slice: x: 4, y: 4 (y_hi: 2, y_lo: 2; y = y_hi * 2 + y_lo), z: 8, core: 2. Of those that a mesh axis runs over, the one named last changes fastest.
Arguments:
- hidden: bfloat16 [2048, 7168], P(('ctx', 'ep')), may hold values from -6 to 6
- q_nope: bfloat16 [2048, 8192], P('ctx', 'ep'), may hold values from -6 to 6
- q_rope: bfloat16 [2048, 4096], P('ctx', 'ep'), may hold values from -100 to 100
- kv_latent: bfloat16 [2048, 512], P('ctx'), may hold values from -6 to 6
- k_rope: bfloat16 [2048, 64], P('ctx'), may hold values from -8 to 8
- key_up: bfloat16 [512, 8192], P(None, 'ep'), may hold values from -0.5 to 0.5
- value_up: bfloat16 [512, 8192], P(None, 'ep'), may hold values from -0.25 to 0.25
- out_proj: bfloat16 [8192, 7168], P(('ep', 'ctx')), may hold values from -0.0625 to 0.0625
- ffn_gain: float32 [7168], replicated, may hold values from 0.5 to 1.5
- router: bfloat16 [7168, 16], replicated, may hold values from -0.0625 to 0.0625
- w_gate: bfloat16 [16, 7168, 2048], P('ep', None, 'ctx'), may hold values from -0.0625 to 0.0625
- w_up: bfloat16 [16, 7168, 2048], P('ep', None, 'ctx'), may hold values from -0.0625 to 0.0625
- w_down: bfloat16 [16, 2048, 7168], P('ep', 'ctx'), may hold values from -0.125 to 0.125
- routes: int32 [2048, 2], P(('ctx', 'ep')), may hold values from 0 to 15, as said below
- load_ema: float32 [16], replicated, may hold values from 0.5 to 1.5
Outputs:
- layer_out: bfloat16 [2048, 7168], P(('ctx', 'ep'))
- new_load: float32 [16], replicated
The draws below stay inside these ranges and needn't reach their ends.
Inputs may be any that keep to these rules, and one draw needn't show every extreme that they name: In the rows of one device every expert that is named is named by exactly 2 routes; a token's routes name different experts.
All inputs are finite; a program needn't handle non-finite values.
Results may differ from the reference program's by a relative error of at most 0.025.
Values may be sent and summed in bfloat16 or wider, within the bound.
A program may use at most 64 MiB of HBM per device.

```python
import jax
import jax.numpy as jnp
from jax import lax

D = 7168
KVL = 512
NOPE = 128
ROPE = 64
VDIM = 128
FFE = 2048
HEAD_DEV = 4
TOP = 2
HEADS = 64
TOK_DEV = 8
SEQ = 2048
EXPERTS = 16
CAP = 2
N_CTX = 16
N_EP = 16


def shared_rotary(key):
    normal_keys = jax.random.normal(jax.random.fold_in(key, 11), (SEQ, ROPE), jnp.float32)
    return normal_keys


def draw_k_rope(key, part):
    normal_keys = shared_rotary(key)
    values = normal_keys
    return values.astype(jnp.bfloat16)


def draw_q_rope(key, part):
    key = jax.random.fold_in(key, 2)
    values = jax.random.normal(key, (SEQ, HEADS * ROPE), jnp.float32)
    return values.astype(jnp.bfloat16)


def draw_routes(key, part):
    key = jax.random.fold_in(key, 3)
    block_count = SEQ // TOK_DEV
    jitter = jax.random.randint(key, (block_count,), 0, max(EXPERTS // 4, 2))
    drift = lax.iota(jnp.int32, block_count) * EXPERTS // block_count
    offsets = drift + jitter
    row_ids = lax.iota(jnp.int32, TOK_DEV)
    route_ids = lax.iota(jnp.int32, TOP)
    ordinal = route_ids[None, :] * TOK_DEV + row_ids[:, None]
    experts = (offsets[:, None, None] + ordinal[None, :, :] // CAP) % EXPERTS
    return experts.reshape(SEQ, TOP).astype(jnp.int32)


def level_of(rng, shape, split, low, top_value):
    def one(position, shards_of):
        steps = jax.random.uniform(jax.random.fold_in(jax.random.fold_in(rng, 6), position), (shards_of,), jnp.float32, low / len(split), top_value / len(split))
        return jnp.repeat(jnp.exp(steps), shape[position] // shards_of).reshape((-1,) + (1,) * (len(shape) - position - 1))

    level = one(*split[0])
    for cut in split[1:]:
        level = level * one(*cut)
    return level


def normal_values(stream_key, dims, deviation, most, pieces=(), dtype=jnp.bfloat16):
    drawn = deviation * jax.random.normal(stream_key, dims, jnp.float32)
    if pieces:
        drawn = drawn * level_of(stream_key, dims, pieces, -0.22, 0.18)
    return jnp.clip(drawn, -most, most).astype(dtype)


def setup_inputs(seed: int = 0) -> dict:
    arg_keys = jax.random.split(jax.random.key(seed), 16)
    hidden = normal_values(arg_keys[0], (SEQ, D), 1.0, 6.0, ((0, 256),))
    q_nope = normal_values(arg_keys[1], (SEQ, HEADS * NOPE), 1.0, 6.0, ((0, 16), (1, 16)))
    q_rope = draw_q_rope(jax.random.fold_in(arg_keys[15], 71), 0)
    kv_latent = normal_values(arg_keys[3], (SEQ, KVL), 1.0, 6.0, ((0, 16),))
    k_rope = draw_k_rope(jax.random.fold_in(arg_keys[15], 71), 0)
    key_up = normal_values(arg_keys[5], (KVL, HEADS * NOPE), NOPE ** -0.5, 0.5, ((1, 16),))
    value_up = normal_values(arg_keys[6], (KVL, HEADS * VDIM), KVL ** -0.5, 0.25, ((1, 16),))
    out_proj = normal_values(arg_keys[7], (HEADS * VDIM, D), (HEADS * VDIM) ** -0.5, 0.0625, ((0, 256),))
    ffn_gain = jnp.clip(1.0 + 0.1 * jax.random.normal(arg_keys[8], (D,), jnp.float32), 0.5, 1.5)
    router = normal_values(arg_keys[9], (D, EXPERTS), D ** -0.5, 0.0625)
    w_gate = normal_values(arg_keys[10], (EXPERTS, D, FFE), D ** -0.5, 0.0625, ((0, 16), (2, 16)))
    w_up = normal_values(arg_keys[11], (EXPERTS, D, FFE), D ** -0.5, 0.0625, ((0, 16), (2, 16)))
    w_down = normal_values(arg_keys[12], (EXPERTS, FFE, D), FFE ** -0.5, 0.125, ((0, 16), (1, 16)))
    routes = draw_routes(jax.random.fold_in(arg_keys[15], 71), 0)
    load_ema = jnp.clip(jax.random.uniform(arg_keys[14], (EXPERTS,), jnp.float32, 0.5, 1.5), 0.5, 1.5)
    return {"hidden": hidden, "q_nope": q_nope, "q_rope": q_rope, "kv_latent": kv_latent, "k_rope": k_rope, "key_up": key_up, "value_up": value_up, "out_proj": out_proj, "ffn_gain": ffn_gain, "router": router, "w_gate": w_gate, "w_up": w_up, "w_down": w_down, "routes": routes, "load_ema": load_ema}


SCORE_FLOOR = -1e+30
NORM_EPS = 1e-06
ROUTE_SCALE = 2.5
LOAD_DECAY = 0.5

def one_head(inputs, kv_latent, k_rope):
    query_nope, query_rope, key_head, value_head = inputs
    score_scale = (NOPE + ROPE) ** (-0.5)
    q_latent = jnp.dot(query_nope, key_head.T, preferred_element_type=jnp.float32).astype(jnp.bfloat16)
    scores = jnp.dot(q_latent, kv_latent.T, preferred_element_type=jnp.float32) + jnp.dot(query_rope, k_rope.T, preferred_element_type=jnp.float32)
    scores = scores * score_scale
    positions = lax.iota(jnp.int32, SEQ)
    allowed = positions[None, :] <= positions[:, None]
    scores = jnp.where(allowed, scores, SCORE_FLOOR)
    top_scores = lax.optimization_barrier(jnp.max(scores, axis=1, keepdims=True))
    exp_scores = jnp.where(allowed, jnp.exp(scores - top_scores), 0.0)
    sum_exp = lax.optimization_barrier(jnp.sum(exp_scores, axis=1, keepdims=True))
    weights = exp_scores.astype(jnp.bfloat16)
    latent_out = (jnp.dot(weights, kv_latent, preferred_element_type=jnp.float32) / sum_exp).astype(jnp.bfloat16)
    return jnp.dot(latent_out, value_head, preferred_element_type=jnp.float32).astype(jnp.bfloat16)

def reference(hidden, q_nope, q_rope, kv_latent, k_rope, key_up, value_up, out_proj, ffn_gain, router, w_gate, w_up, w_down, routes, load_ema):
    head_inputs = (q_nope.reshape(SEQ, HEADS, NOPE).transpose(1, 0, 2), q_rope.reshape(SEQ, HEADS, ROPE).transpose(1, 0, 2), key_up.reshape(KVL, HEADS, NOPE).transpose(1, 0, 2), value_up.reshape(KVL, HEADS, VDIM).transpose(1, 0, 2))
    head_out = lax.map(lambda inputs: one_head(inputs, kv_latent, k_rope), head_inputs)
    head_cols = head_out.transpose(1, 0, 2).reshape(SEQ, HEADS * VDIM)
    group_width = HEAD_DEV * VDIM
    attn_sum = jnp.zeros((SEQ, D), jnp.float32)
    for group_index in range(N_EP):
        columns = head_cols[:, group_index * group_width:(group_index + 1) * group_width]
        weight_rows = out_proj[group_index * group_width:(group_index + 1) * group_width]
        group_term = jnp.dot(columns, weight_rows, preferred_element_type=jnp.float32).astype(jnp.bfloat16)
        attn_sum = attn_sum + lax.optimization_barrier(group_term).astype(jnp.float32)
    residual = (hidden.astype(jnp.float32) + attn_sum).astype(jnp.bfloat16)
    residual_wide = residual.astype(jnp.float32)
    mean_square = lax.optimization_barrier(jnp.mean(residual_wide * residual_wide, axis=1, keepdims=True))
    normed = (residual_wide * lax.rsqrt(mean_square + NORM_EPS) * ffn_gain).astype(jnp.bfloat16)
    affinity = jax.nn.sigmoid(jnp.dot(normed, router, preferred_element_type=jnp.float32))
    chosen = jnp.take_along_axis(affinity, routes, axis=1)
    gate_weights = ROUTE_SCALE * chosen / lax.optimization_barrier(jnp.sum(chosen, axis=1, keepdims=True))
    pair_expert = routes.reshape(-1).astype(jnp.int32)
    pair_count = SEQ * TOP
    row_bound = N_CTX * N_EP * CAP
    slice_width = FFE // N_CTX

    def one_expert(expert_index):
        matches = jnp.nonzero(pair_expert == expert_index, size=row_bound, fill_value=pair_count)[0].astype(jnp.int32)
        token_rows = jnp.take(normed, jnp.minimum(matches, pair_count - 1) // TOP, axis=0)
        gate_part = jnp.dot(token_rows, w_gate[expert_index], preferred_element_type=jnp.float32)
        up_part = jnp.dot(token_rows, w_up[expert_index], preferred_element_type=jnp.float32)
        activations = (jax.nn.silu(gate_part) * up_part).astype(jnp.bfloat16)
        expert_sum = jnp.zeros((row_bound, D), jnp.float32)
        for slice_index in range(N_CTX):
            lower_edge = slice_index * slice_width
            slice_term = jnp.dot(activations[:, lower_edge:lower_edge + slice_width], w_down[expert_index, lower_edge:lower_edge + slice_width], preferred_element_type=jnp.float32)
            expert_sum = expert_sum + lax.optimization_barrier(slice_term.astype(jnp.bfloat16)).astype(jnp.float32)
        return (expert_sum.astype(jnp.bfloat16), matches)
    expert_rows, expert_matches = lax.map(one_expert, lax.iota(jnp.int32, EXPERTS))
    pair_out = jnp.zeros((pair_count, D), jnp.float32).at[expert_matches.reshape(-1)].add(expert_rows.reshape(-1, D).astype(jnp.float32), mode='drop')
    routed_sum = lax.optimization_barrier(jnp.sum(gate_weights[:, :, None] * pair_out.reshape(SEQ, TOP, D), axis=1))
    layer_out = (residual_wide + routed_sum).astype(jnp.bfloat16)
    expert_load = lax.optimization_barrier(jnp.sum((pair_expert[:, None] == lax.iota(jnp.int32, EXPERTS)[None, :]).astype(jnp.float32), axis=0))
    mean_load = pair_count / EXPERTS
    new_load = LOAD_DECAY * load_ema + (1.0 - LOAD_DECAY) * expert_load / mean_load
    return (layer_out, new_load)
```

```python
import functools

import jax
import jax.numpy as jnp
from jax import lax
from jax.experimental import pallas as pl
from jax.experimental.pallas import tpu as pltpu
from jax.sharding import PartitionSpec as P

D = 7168
KVL = 512
NOPE = 128
ROPE = 64
VDIM = 128
HEAD_DEV = 4
SL = 896
EXPERTS = 16
META = 128

SCORE_FLOOR = -1e30
NORM_EPS = 1e-06
ROUTE_SCALE = 2.5
LOAD_DECAY = 0.5
MESH = pl.DeviceIdType.MESH
BF = jnp.bfloat16
F32 = jnp.float32
VMEM_LIMIT = 56 * 2**20


def place():
    c = lax.axis_index("ctx")
    e = lax.axis_index("ep")
    return c, e, lax.div(c, 8), lax.rem(c, 8), lax.div(e, 2), lax.rem(e, 2)


def remote(src, dst, send, recv, device):
    return pltpu.make_async_remote_copy(
        src_ref=src, dst_ref=dst, send_sem=send, recv_sem=recv, device_id=device, device_id_type=MESH
    )


def dot(a, b):
    return jnp.dot(a, b, preferred_element_type=F32)


def dot_t(a, b):
    return lax.dot_general(a, b, (((1,), (1,)), ((), ())), preferred_element_type=F32)


def iota(shape, dim):
    return lax.broadcasted_iota(jnp.int32, shape, dim)


def selector(rows, columns, shift, width):
    row, column = iota((rows, columns), 0), iota((rows, columns), 1)
    return jnp.where((row == column + shift) & (column < width), 1.0, 0.0).astype(BF)


def column_of(block, index):
    return jnp.sum(jnp.where(iota(block.shape, 1) == index, block, 0.0), axis=1, keepdims=True)


def attention_kernel(
    q_nope, q_rope, kv, k_rope, key_up, value_up, out_proj, hidden, routes, w_gate, w_up,
    attn_out, hidden_out, wgu,
    KV, Q, top, total, accum, HO, WO, PB, SB, RED, RK, TS, TR, HS, HR,
    kv_s, kv_r, kf_s, kf_r, op_s, op_r, hd_s, hd_r, w_s, w_r, wf_s, wf_r,
    hp_s, hm_s, ho_r, sb_s, sb_r, rk_s, rk_r, t_s, t_r, local,
):
    c, e, yl, z, k, s = place()
    sib = 2 * k + 1 - s
    e_half, e_row = lax.div(e, 8), lax.rem(e, 8)
    turned = (yl * 8 + k, 2 * z + s)

    KV[pl.ds(pl.multiple_of(c * 128, 128), 128), 0:KVL] = kv[...]
    KV[pl.ds(pl.multiple_of(c * 128, 128), 128), KVL:640] = dot(
        k_rope[...], selector(ROPE, 128, 0, ROPE)
    ).astype(BF)

    @pl.when(lax.rem(c, 2) == 0)
    def _():
        KV[pl.ds(pl.multiple_of((c + 1) * 128, 128), 128), :] = jnp.zeros((128, 640), BF)

    route_block = jnp.where(
        iota((8, META), 1) == 0,
        routes[:, 0:1],
        jnp.where(iota((8, META), 1) == 1, routes[:, 1:2], 0),
    ).astype(F32)
    for kk in range(8):
        HS[kk, :, 0:SL] = hidden[:, kk * SL : (kk + 1) * SL].astype(F32)
        HS[kk, :, SL:1024] = route_block

    barrier = pltpu.get_barrier_semaphore()
    for d in range(1, 16):
        pl.semaphore_signal(barrier, 1, device_id=(lax.rem(c + d, 16), e), device_id_type=MESH)
        pl.semaphore_signal(barrier, 1, device_id=(c, lax.rem(e + d, 16)), device_id_type=MESH)

    @pl.when(z != k)
    def _():
        pl.semaphore_signal(barrier, 1, device_id=turned, device_id_type=MESH)

    pl.semaphore_wait(barrier, 30 + (z != k).astype(jnp.int32))

    def kv_copy(d):
        half = KV.at[pl.ds(pl.multiple_of(c * 128 + s * 64, 64), 64), :]
        return remote(half, half, kv_s.at[d], kv_r.at[c], (c + d, e))

    for d in range(1, 16):

        @pl.when(c + d < 16)
        def _():
            kv_copy(d).start()

    def hidden_copy(kk):
        return remote(
            HS.at[kk], HR.at[e_row], hd_s.at[kk], hd_r.at[e_row], (c, 2 * kk + e_half)
        )

    for kk in range(8):

        @pl.when(2 * kk + e_half != e)
        def _():
            hidden_copy(kk).start()

        @pl.when(2 * kk + e_half == e)
        def _():
            HR[e_row] = HS[kk]

    def proj_copy(d):
        cc = lax.rem(c + d, 16)
        zz = lax.rem(cc, 8)
        return remote(
            out_proj.at[:, pl.ds(pl.multiple_of(zz * SL, 128), SL)],
            WO.at[pl.ds(pl.multiple_of(c * 32, 32), 32), :],
            op_s.at[d],
            op_r.at[c],
            (cc, e),
        )

    own_proj = pltpu.make_async_copy(
        out_proj.at[:, pl.ds(pl.multiple_of(z * SL, 128), SL)],
        WO.at[pl.ds(pl.multiple_of(c * 32, 32), 32), :],
        local.at[0],
    )
    own_proj.start()
    for d in range(1, 16):
        proj_copy(d).start()

    def weight_copy(d, which):
        kk = lax.rem(k + d, 8)
        source = (w_gate, w_up)[which]
        return remote(
            source.at[0, pl.ds(pl.multiple_of(kk * SL, SL), SL), :],
            wgu.at[e, :, pl.ds(which * 128, 128)],
            w_s.at[d, which],
            w_r.at[k, which],
            (c, 2 * kk + s),
        )

    def own_weight(which):
        source = (w_gate, w_up)[which]
        return pltpu.make_async_copy(
            source.at[0, pl.ds(pl.multiple_of(k * SL, SL), SL), :],
            wgu.at[e, :, pl.ds(which * 128, 128)],
            local.at[1 + which],
        )

    for which in range(2):
        own_weight(which).start()
    for d in range(1, 8):
        for which in range(2):
            weight_copy(d, which).start()

    for h in range(HEAD_DEV):
        rows, columns = slice(h * 128, (h + 1) * 128), slice(h * 128, (h + 1) * 128)
        Q[rows, 0:KVL] = dot_t(q_nope[:, columns], key_up[:, columns]).astype(BF)
        Q[rows, KVL:640] = dot(
            q_rope[...], selector(HEAD_DEV * ROPE, 128, h * ROPE, ROPE)
        ).astype(BF)
    top[...] = jnp.full(top.shape, SCORE_FLOOR, F32)
    total[...] = jnp.zeros(total.shape, F32)
    accum[...] = jnp.zeros(accum.shape, F32)

    def half_block(j, core):
        return KV.at[pl.ds(pl.multiple_of(j * 128 + core * 64, 64), 64), :]

    def kv_forward(j, core):
        half = half_block(j, core)
        return remote(half, half, kf_s.at[j], kf_r.at[j], (c, sib))

    def pass_on(p):
        for j in (2 * p + 1, 2 * p):

            @pl.when((p >= 0) & (j < c))
            def _():
                half = half_block(j, s)
                remote(half, half, kv_s.at[0], kv_r.at[j], (c, e)).wait_recv()
                kv_forward(j, s).start()

    score_scale = (NOPE + ROPE) ** (-0.5)

    def attend(p):
        for j in (2 * p + 1, 2 * p):

            @pl.when(j < c)
            def _():
                kv_forward(j, 1 - s).wait_recv()

        keys = KV[pl.ds(pl.multiple_of(p * 256, 256), 256), :]
        scores = dot_t(Q[...], keys)
        query_pos = c * 128 + (iota(scores.shape, 0) & 127)
        key_pos = p * 256 + iota(scores.shape, 1)
        scores = jnp.where(key_pos <= query_pos, scores, SCORE_FLOOR)
        top_old = top[...]
        top_new = jnp.maximum(top_old, jnp.max(scores, axis=1, keepdims=True))
        exp_scores = jnp.exp((scores - top_new) * score_scale)
        shrink = jnp.exp((top_old - top_new) * score_scale)
        top[...] = top_new
        total[...] = total[...] * shrink + jnp.sum(exp_scores, axis=1, keepdims=True)
        accum[...] = accum[...] * shrink + dot(exp_scores.astype(BF), keys[:, 0:KVL])

    last = lax.div(c, 2)
    pass_on(last)
    pass_on(last - 1)

    def attention_step(i, carry):
        attend(last - i)
        pass_on(last - i - 2)
        return carry

    lax.fori_loop(0, last + 1, attention_step, 0)

    own_rows = pl.ds(pl.multiple_of(z * 128, 128), 128)
    for h in range(HEAD_DEV):
        rows, columns = slice(h * 128, (h + 1) * 128), slice(h * 128, (h + 1) * 128)
        latent = (accum[rows, :] / total[rows, :]).astype(BF)
        HO[own_rows, columns] = dot(latent, value_up[:, columns]).astype(BF)

    def ho_copy(zz, half, up):
        block = HO.at[pl.ds(pl.multiple_of(zz * 128 + half * 64, 64), 64), :]
        target = yl * 8 + lax.rem(z + (1 if up else 7), 8)
        return remote(
            block, block, (hp_s if up else hm_s).at[zz, half], ho_r.at[zz, half], (target, e)
        )

    for half in range(2):
        ho_copy(z, half, True).start()
        ho_copy(z, half, False).start()
    own_proj.wait()
    for d in range(1, 16):
        cc = lax.rem(c + d, 16)
        remote(
            out_proj.at[:, pl.ds(0, SL)],
            WO.at[pl.ds(pl.multiple_of(cc * 32, 32), 32), :],
            op_s.at[0],
            op_r.at[cc],
            (c, e),
        ).wait_recv()

    def sib_copy(zz, core):
        return remote(
            PB.at[zz, pl.ds(pl.multiple_of((1 - core) * 64, 64), 64), :],
            SB.at[zz],
            sb_s.at[zz],
            sb_r.at[zz],
            (c, sib),
        )

    def project(zz):
        PB[zz] = dot(HO[pl.ds(pl.multiple_of(zz * 128, 128), 128), :], WO[...]).astype(BF)
        sib_copy(zz, s).start()

    def chip_copy(zz):
        return remote(RED.at[zz], RK.at[k], rk_s.at[zz], rk_r.at[k], (c, 2 * zz + s))

    def reduce_pair(zz):
        sib_copy(zz, s).wait_recv()
        own = PB[zz, pl.ds(pl.multiple_of(s * 64, 64), 64), :]
        RED[zz] = (own.astype(F32) + SB[zz].astype(F32)).astype(BF)

        @pl.when(zz != k)
        def _():
            chip_copy(zz).start()

        @pl.when(zz == k)
        def _():
            RK[k] = RED[zz]

    project(z)
    waiting = z
    for t in range(1, 5):
        below, above = lax.rem(z + 8 - t, 8), lax.rem(z + t, 8)
        for half in range(2):
            ho_copy(below, half, True).wait_recv()
            if t < 4:
                ho_copy(below, half, True).start()
        project(below)
        reduce_pair(waiting)
        waiting = below
        if t < 4:
            for half in range(2):
                ho_copy(above, half, False).wait_recv()
                if t < 3:
                    ho_copy(above, half, False).start()
            project(above)
            reduce_pair(waiting)
            waiting = above
    reduce_pair(waiting)

    for d in range(1, 8):
        kk = lax.rem(k + d, 8)
        remote(RED.at[0], RK.at[kk], rk_s.at[0], rk_r.at[kk], (c, e)).wait_recv()
    summed = RK[0].astype(F32)
    for kk in range(1, 8):
        summed = summed + RK[kk].astype(F32)
    TS[...] = summed.astype(BF)

    def turn_copy():
        return remote(TS, TR, t_s.at[0], t_r.at[0], turned)

    @pl.when(z != k)
    def _():
        turn_copy().start()

    for which in range(2):
        own_weight(which).wait()

    def forward_copy(kk, core):
        expert = 2 * kk + core
        return remote(wgu.at[expert], wgu.at[expert], wf_s.at[kk], wf_r.at[kk], (c, sib))

    forward_copy(k, s).start()
    for d in range(1, 8):
        kk = lax.rem(k + d, 8)
        for which in range(2):
            piece = wgu.at[2 * kk + s, :, pl.ds(which * 128, 128)]
            remote(piece, piece, w_s.at[0, which], w_r.at[kk, which], (c, e)).wait_recv()
        forward_copy(kk, s).start()

    for j in range(8):

        @pl.when(8 * s + j != e)
        def _():
            remote(HS.at[0], HR.at[j], hd_s.at[0], hd_r.at[j], (c, e)).wait_recv()

    hidden_out[...] = HR[...].reshape(64, 1024)

    @pl.when(z != k)
    def _():
        turn_copy().wait_recv()
        attn_out[...] = TR[...]

    @pl.when(z == k)
    def _():
        attn_out[...] = TS[...]

    for kk in range(8):
        forward_copy(kk, 1 - s).wait_recv()

    for d in range(1, 16):

        @pl.when(c + d < 16)
        def _():
            kv_copy(d).wait_send()

        proj_copy(d).wait_send()

    for j in range(15):

        @pl.when(j < c)
        def _():
            kv_forward(j, s).wait_send()

    for kk in range(8):

        @pl.when(2 * kk + e_half != e)
        def _():
            hidden_copy(kk).wait_send()

        forward_copy(kk, s).wait_send()
        sib_copy(kk, s).wait_send()

        @pl.when(kk != k)
        def _():
            chip_copy(kk).wait_send()

    for d in range(1, 8):
        for which in range(2):
            weight_copy(d, which).wait_send()
    for half in range(2):
        for t in range(0, 4):
            ho_copy(lax.rem(z + 8 - t, 8), half, True).wait_send()
        for t in range(0, 3):
            ho_copy(lax.rem(z + t, 8), half, False).wait_send()

    @pl.when(z != k)
    def _():
        turn_copy().wait_send()


def experts_kernel(
    attn, hidden, router, gain, wgu, w_down,
    act_out, meta_out, residual_out, wd,
    X, W, RT, GN, ST, XC, acc0, acc1, HS, HR, A,
    local, st_s, st_r, w_s, w_r, wf_s, wf_r, xp_s, xm_s, xy_s, x_r, h_s, h_r, a_s, a_r,
):
    c, e, yl, z, k, s = place()
    sib = 2 * k + 1 - s
    c_y = (1 - yl) * 8 + z
    c_up = yl * 8 + lax.rem(z + 1, 8)
    c_down = yl * 8 + lax.rem(z + 7, 8)

    fetch_router = pltpu.make_async_copy(
        router.at[pl.ds(pl.multiple_of(k * SL, SL), SL), :], RT, local.at[0]
    )
    fetch_gain = pltpu.make_async_copy(gain.at[k], GN, local.at[1])
    fetch_wgu = pltpu.make_async_copy(wgu, W, local.at[2])
    own_down = pltpu.make_async_copy(
        w_down.at[0, :, pl.ds(pl.multiple_of(k * SL, 128), SL)],
        wd.at[pl.ds(pl.multiple_of(e * 128, 128), 128), :],
        local.at[3],
    )
    fetch_router.start()
    fetch_gain.start()
    own_down.start()

    barrier = pltpu.get_barrier_semaphore()
    for d in range(1, 8):
        pl.semaphore_signal(
            barrier, 1, device_id=(c, 2 * lax.rem(k + d, 8) + s), device_id_type=MESH
        )
    pl.semaphore_signal(barrier, 1, device_id=(c, sib), device_id_type=MESH)
    for neighbour in (c_y, c_up, c_down):
        pl.semaphore_signal(barrier, 1, device_id=(neighbour, e), device_id_type=MESH)
    fetch_router.wait()
    fetch_gain.wait()
    fetch_wgu.start()

    residual = (hidden[:, 0:SL] + attn[...].astype(F32)).astype(BF).astype(F32)
    residual_out[...] = residual
    gains = GN[...]
    lane = iota((64, META), 1)
    padded_router = dot(RT[...], selector(EXPERTS, META, 0, EXPERTS)).astype(BF)
    logits = dot((residual * gains).astype(BF), padded_router)
    squares = jnp.sum(residual * residual, axis=1, keepdims=True)
    ST[k] = jnp.where(lane == EXPERTS, squares, logits)
    pl.semaphore_wait(barrier, 11)

    def stat_copy(d):
        kk = lax.rem(k + d, 8)
        return remote(ST.at[k], ST.at[k], st_s.at[d], st_r.at[k], (c, 2 * kk + s))

    for d in range(1, 8):
        stat_copy(d).start()

    def down_copy(d):
        kk = lax.rem(k + d, 8)
        return remote(
            w_down.at[0, :, pl.ds(pl.multiple_of(kk * SL, 128), SL)],
            wd.at[pl.ds(pl.multiple_of(e * 128, 128), 128), :],
            w_s.at[d],
            w_r.at[k],
            (c, 2 * kk + s),
        )

    for d in range(1, 8):
        down_copy(d).start()
    for d in range(1, 8):
        kk = lax.rem(k + d, 8)
        remote(ST.at[kk], ST.at[kk], st_s.at[0], st_r.at[kk], (c, e)).wait_recv()
    stats = ST[0]
    for kk in range(1, 8):
        stats = stats + ST[kk]
    inverse = lax.rsqrt(column_of(stats, EXPERTS) / D + NORM_EPS)
    normed = (residual * inverse * gains).astype(BF)
    affinity = 1.0 / (1.0 + jnp.exp(-(stats * inverse)))
    routed = hidden[:, SL:1024]
    route0, route1 = column_of(routed, 0), column_of(routed, 1)
    lane_f = lane.astype(F32)
    chosen0 = jnp.sum(jnp.where(lane_f == route0, affinity, 0.0), axis=1, keepdims=True)
    chosen1 = jnp.sum(jnp.where(lane_f == route1, affinity, 0.0), axis=1, keepdims=True)
    scale = ROUTE_SCALE / (chosen0 + chosen1)
    meta = jnp.where(lane == 0, route0, jnp.where(lane == 1, route1, 0.0))
    for index, weight in ((2, chosen0 * scale), (4, chosen1 * scale)):
        coarse = weight.astype(BF).astype(F32)
        meta = jnp.where(lane == index, coarse, meta)
        meta = jnp.where(lane == index + 1, weight - coarse, meta)

    def rows_of(cc):
        return pl.ds(pl.multiple_of(cc * 64, 64), 64)

    X[rows_of(c), 0:SL] = normed
    X[rows_of(c), SL:1024] = meta.astype(BF)

    def row_copy(cc, way):
        block = X.at[rows_of(cc), :]
        target = {"y": c_y, "up": c_up, "down": c_down}[way]
        sems = {"y": xy_s, "up": xp_s, "down": xm_s}[way]
        return remote(block, block, sems.at[cc], x_r.at[cc], (target, e))

    row_copy(c, "y").start()
    row_copy(c, "up").start()
    row_copy(c, "down").start()
    row_copy(c_y, "y").wait_recv()
    row_copy(c_y, "up").start()
    row_copy(c_y, "down").start()

    def block_of(y, zz):
        return y * 8 + zz

    def arrive(zz, way, go_on):
        for y in (yl, 1 - yl):
            row_copy(block_of(y, zz), way).wait_recv()
            if go_on:
                row_copy(block_of(y, zz), way).start()

    def half_copy(zz):
        return remote(HS.at[zz], HR.at[k], h_s.at[zz], h_r.at[k], (c, 2 * zz + s))

    def first_layers(za, zb):
        places = [(0, za), (1, za), (0, zb), (1, zb)]
        for i, (y, zz) in enumerate(places):
            XC[i * 64 : (i + 1) * 64, :] = X[rows_of(block_of(y, zz)), :]
        acc0[...] = jnp.zeros(acc0.shape, F32)
        acc1[...] = jnp.zeros(acc1.shape, F32)
        routed_here = XC[:, SL:1024].astype(F32)
        r0, r1 = column_of(routed_here, 0), column_of(routed_here, 1)

        def one_expert(expert, carry):
            part = dot(XC[:, 0:SL], W[expert])
            number = expert.astype(F32)
            acc0[...] += jnp.where(r0 == number, part, 0.0)
            acc1[...] += jnp.where(r1 == number, part, 0.0)
            return carry

        lax.fori_loop(0, EXPERTS, one_expert, 0)
        for i, (y, zz) in enumerate(places):
            HS[zz, y, 0] = acc0[i * 64 : (i + 1) * 64, :].astype(BF)
            HS[zz, y, 1] = acc1[i * 64 : (i + 1) * 64, :].astype(BF)
        for zz in (za, zb):

            @pl.when(zz != k)
            def _():
                half_copy(zz).start()

            @pl.when(zz == k)
            def _():
                HR[k] = HS[zz]

    near = [lax.rem(z + 8 - t, 8) for t in range(5)]
    far = [lax.rem(z + t, 8) for t in range(4)]
    arrive(near[1], "up", True)
    arrive(far[1], "down", True)
    fetch_wgu.wait()
    first_layers(z, near[1])
    arrive(near[2], "up", True)
    arrive(far[2], "down", True)
    first_layers(far[1], near[2])
    arrive(near[3], "up", True)
    arrive(far[3], "down", False)
    first_layers(far[2], near[3])
    arrive(near[4], "up", False)
    first_layers(far[3], near[4])
    meta_out[...] = X[:, SL:1024]

    for d in range(1, 8):
        kk = lax.rem(k + d, 8)
        remote(HS.at[0], HR.at[kk], h_s.at[0], h_r.at[kk], (c, e)).wait_recv()
    for y in range(2):
        meta_here = X[rows_of(block_of(y, k)), SL:1024].astype(F32)
        for r in range(2):
            both = HR[0, y, r].astype(F32)
            for kk in range(1, 8):
                both = both + HR[kk, y, r].astype(F32)
            weight = column_of(meta_here, 2 + 2 * r) + column_of(meta_here, 3 + 2 * r)
            gate, up = both[:, 0:128], both[:, 128:256]
            A[k, y, r] = (gate / (1.0 + jnp.exp(-gate)) * up * weight).astype(BF)

    def act_copy(d):
        kk = lax.rem(k + d, 8)
        return remote(A.at[k], A.at[k], a_s.at[d], a_r.at[k], (c, 2 * kk + s))

    for d in range(1, 8):
        act_copy(d).start()

    own_down.wait()

    def forward_copy(kk, core):
        block = wd.at[pl.ds(pl.multiple_of((2 * kk + core) * 128, 128), 128), :]
        return remote(block, block, wf_s.at[kk], wf_r.at[kk], (c, sib))

    forward_copy(k, s).start()
    for d in range(1, 8):
        kk = lax.rem(k + d, 8)
        block = wd.at[pl.ds(pl.multiple_of((2 * kk + s) * 128, 128), 128), :]
        remote(block, block, w_s.at[0], w_r.at[kk], (c, e)).wait_recv()
        forward_copy(kk, s).start()
    for d in range(1, 8):
        kk = lax.rem(k + d, 8)
        remote(A.at[kk], A.at[kk], a_s.at[0], a_r.at[kk], (c, e)).wait_recv()
    act_out[...] = A[...]
    for kk in range(8):
        forward_copy(kk, 1 - s).wait_recv()

    for d in range(1, 8):
        stat_copy(d).wait_send()
        down_copy(d).wait_send()
        act_copy(d).wait_send()
    for kk in range(8):
        forward_copy(kk, s).wait_send()

        @pl.when(kk != k)
        def _():
            half_copy(kk).wait_send()

    row_copy(c, "y").wait_send()
    for y in (yl, 1 - yl):
        for t in range(4):
            row_copy(block_of(y, near[t]), "up").wait_send()
        for t in range(3):
            row_copy(block_of(y, far[t]), "down").wait_send()


def down_kernel(
    act, meta, residual, wd, ema,
    layer_out, load_out,
    WD, AC, DP, RP, RM, SP, SM, YS, YR, OS, OR, CS, CR,
    local, p_s, p_r, m_s, m_r, y_s, y_r, o_s, o_r, c_s, c_r,
):
    c, e, yl, z, k, s = place()
    sib = 2 * k + 1 - s
    c_y = (1 - yl) * 8 + z
    c_up = yl * 8 + lax.rem(z + 1, 8)
    c_down = yl * 8 + lax.rem(z + 7, 8)
    e_half = lax.div(e, 8)

    fetch = pltpu.make_async_copy(wd, WD, local.at[0])
    fetch.start()
    barrier = pltpu.get_barrier_semaphore()
    pl.semaphore_signal(barrier, 1, device_id=(c, sib), device_id_type=MESH)
    for neighbour in (c_y, c_up, c_down):
        pl.semaphore_signal(barrier, 1, device_id=(neighbour, e), device_id_type=MESH)
    for kk in range(8):

        @pl.when(2 * kk + e_half != e)
        def _():
            pl.semaphore_signal(barrier, 1, device_id=(c, 2 * kk + e_half), device_id_type=MESH)

    pl.semaphore_wait(barrier, 12 - (e_half == s).astype(jnp.int32))

    routed = meta[...].astype(F32)
    lane_f = iota(routed.shape, 1).astype(F32)
    named = jnp.where(lane_f == column_of(routed, 0), 1.0, 0.0) + jnp.where(
        lane_f == column_of(routed, 1), 1.0, 0.0
    )
    CS[...] = jnp.broadcast_to(jnp.sum(named, axis=0, keepdims=True), CS.shape)
    count_copy = remote(CS, CR, c_s.at[0], c_r.at[0], (c, sib))
    count_copy.start()
    fetch.wait()

    def second_layer(za, zb):
        places = [(0, za), (1, za), (0, zb), (1, zb)]
        for i, (y, zz) in enumerate(places):
            rows = slice(i * 64, (i + 1) * 64)
            here = meta[pl.ds(pl.multiple_of((y * 8 + zz) * 64, 64), 64), :].astype(F32)
            r0, r1 = column_of(here, 0), column_of(here, 1)
            a0, a1 = act[zz, y, 0].astype(F32), act[zz, y, 1].astype(F32)
            for expert in range(EXPERTS):
                picked = jnp.where(r0 == float(expert), a0, 0.0) + jnp.where(
                    r1 == float(expert), a1, 0.0
                )
                AC[rows, expert * 128 : (expert + 1) * 128] = picked.astype(BF)
        out = dot(AC[...], WD[...])
        for i, (y, zz) in enumerate(places):
            DP[zz, y] = out[i * 64 : (i + 1) * 64, :].astype(BF)

    def up_copy(source, step, y):
        return remote(source, RP.at[step, y], p_s.at[step, y], p_r.at[step, y], (c_up, e))

    def down_copy(source, step, y):
        return remote(source, RM.at[step, y], m_s.at[step, y], m_r.at[step, y], (c_down, e))

    ups = [lax.rem(z + 4 - t, 8) for t in range(5)]
    downs = [lax.rem(z + 5 + t, 8) for t in range(4)]
    second_layer(ups[0], downs[0])
    for y in range(2):
        up_copy(DP.at[ups[0], y], 0, y).start()
        down_copy(DP.at[downs[0], y], 0, y).start()
    for t in range(1, 4):
        second_layer(ups[t], downs[t])
        for y in range(2):
            up_copy(SP.at[0, y], t - 1, y).wait_recv()
            SP[t - 1, y] = (DP[ups[t], y].astype(F32) + RP[t - 1, y].astype(F32)).astype(BF)
            up_copy(SP.at[t - 1, y], t, y).start()
            if t < 3:
                down_copy(SM.at[0, y], t - 1, y).wait_recv()
                SM[t - 1, y] = (DP[downs[t], y].astype(F32) + RM[t - 1, y].astype(F32)).astype(BF)
                down_copy(SM.at[t - 1, y], t, y).start()

    def final(y):
        return DP[z, y].astype(F32) + RP[3, y].astype(F32) + RM[2, y].astype(F32)

    for y in (1 - yl, yl):
        down_copy(SM.at[0, 0], 2, y).wait_recv()
        up_copy(SP.at[0, 0], 3, y).wait_recv()
        if y is yl:
            break
        YS[...] = final(y).astype(BF)
        y_copy = remote(YS, YR, y_s.at[0], y_r.at[0], (c_y, e))
        y_copy.start()
    own = final(yl) + residual[...]
    y_copy.wait_recv()
    OS[...] = own + YR[...].astype(F32)

    def owner_copy(j):
        return remote(
            OS.at[pl.ds(j * 8, 8), :], OR.at[k], o_s.at[j], o_r.at[k], (c, 8 * s + j)
        )

    for j in range(8):

        @pl.when(8 * s + j != e)
        def _():
            owner_copy(j).start()

        @pl.when(8 * s + j == e)
        def _():
            OR[k] = OS[pl.ds(j * 8, 8), :]

    count_copy.wait_recv()
    counts = (CS[...] + CR[...])[0:1, 0:EXPERTS]
    load_out[...] = LOAD_DECAY * ema[...] + (1.0 - LOAD_DECAY) * counts / 256.0

    for kk in range(8):

        @pl.when(2 * kk + e_half != e)
        def _():
            remote(
                OS.at[pl.ds(0, 8), :], OR.at[kk], o_s.at[0], o_r.at[kk], (c, e)
            ).wait_recv()

        layer_out[:, kk * SL : (kk + 1) * SL] = OR[kk].astype(BF)

    for y in range(2):
        up_copy(DP.at[ups[0], y], 0, y).wait_send()
        down_copy(DP.at[downs[0], y], 0, y).wait_send()
        for t in range(1, 4):
            up_copy(SP.at[t - 1, y], t, y).wait_send()
            if t < 3:
                down_copy(SM.at[t - 1, y], t, y).wait_send()
    y_copy.wait_send()
    count_copy.wait_send()
    for j in range(8):

        @pl.when(8 * s + j != e)
        def _():
            owner_copy(j).wait_send()


def in_vmem(count):
    return [pl.BlockSpec(memory_space=pltpu.VMEM)] * count


def anywhere(count):
    return [pl.BlockSpec(memory_space=pl.ANY)] * count


def dma(*shape):
    return pltpu.SemaphoreType.DMA(shape)


def shaped(shape, dtype):
    return jax.ShapeDtypeStruct(shape, dtype)


def params(number):
    return pltpu.CompilerParams(
        collective_id=number, has_side_effects=True, vmem_limit_bytes=VMEM_LIMIT
    )


def body(
    hidden, q_nope, q_rope, kv_latent, k_rope, key_up, value_up, out_proj, ffn_gain, router,
    w_gate, w_up, w_down, routes, load_ema,
):
    v = pltpu.VMEM
    attn, rows, wgu = pl.pallas_call(
        attention_kernel,
        out_shape=(shaped((64, SL), BF), shaped((64, 1024), F32), shaped((16, SL, 256), BF)),
        in_specs=in_vmem(6) + anywhere(1) + in_vmem(2) + anywhere(2),
        out_specs=tuple(in_vmem(2) + anywhere(1)),
        scratch_shapes=[
            v((2048, 640), BF), v((512, 640), BF), v((512, 1), F32), v((512, 1), F32),
            v((512, 512), F32), v((1024, 512), BF), v((512, SL), BF), v((8, 128, SL), BF),
            v((8, 64, SL), BF), v((8, 64, SL), BF), v((8, 64, SL), BF), v((64, SL), BF),
            v((64, SL), BF), v((8, 8, 1024), F32), v((8, 8, 1024), F32),
            dma(16), dma(16), dma(16), dma(16), dma(16), dma(16), dma(8), dma(8),
            dma(8, 2), dma(8, 2), dma(8), dma(8), dma(8, 2), dma(8, 2), dma(8, 2),
            dma(8), dma(8), dma(8), dma(8), dma(1), dma(1), dma(3),
        ],
        compiler_params=params(0),
        name="attention",
    )(q_nope, q_rope, kv_latent, k_rope, key_up, value_up, out_proj, hidden, routes, w_gate, w_up)
    act, meta, residual, wd = pl.pallas_call(
        experts_kernel,
        out_shape=(
            shaped((8, 2, 2, 64, 128), BF),
            shaped((1024, META), BF),
            shaped((64, SL), F32),
            shaped((2048, SL), BF),
        ),
        in_specs=in_vmem(2) + anywhere(4),
        out_specs=tuple(in_vmem(3) + anywhere(1)),
        scratch_shapes=[
            v((1024, 1024), BF), v((16, SL, 256), BF), v((SL, EXPERTS), BF), v((1, SL), F32),
            v((8, 64, META), F32), v((256, 1024), BF), v((256, 256), F32), v((256, 256), F32),
            v((8, 2, 2, 64, 256), BF), v((8, 2, 2, 64, 256), BF), v((8, 2, 2, 64, 128), BF),
            dma(4), dma(8), dma(8), dma(8), dma(8), dma(8), dma(8), dma(16), dma(16), dma(16),
            dma(16), dma(8), dma(8), dma(8), dma(8),
        ],
        compiler_params=params(1),
        name="experts",
    )(attn, rows, router, ffn_gain.reshape(8, 1, SL), wgu, w_down)
    layer_out, new_load = pl.pallas_call(
        down_kernel,
        out_shape=(shaped((8, D), BF), shaped((1, EXPERTS), F32)),
        in_specs=in_vmem(3) + anywhere(1) + in_vmem(1),
        out_specs=tuple(in_vmem(2)),
        scratch_shapes=[
            v((2048, SL), BF), v((256, 2048), BF), v((8, 2, 64, SL), BF), v((4, 2, 64, SL), BF),
            v((3, 2, 64, SL), BF), v((3, 2, 64, SL), BF), v((2, 2, 64, SL), BF), v((64, SL), BF),
            v((64, SL), BF), v((64, SL), F32), v((8, 8, SL), F32), v((8, 128), F32),
            v((8, 128), F32),
            dma(1), dma(4, 2), dma(4, 2), dma(3, 2), dma(3, 2), dma(1), dma(1), dma(8), dma(8),
            dma(1), dma(1),
        ],
        compiler_params=params(2),
        name="second_layer",
    )(act, meta, residual, wd, load_ema.reshape(1, EXPERTS))
    return layer_out, new_load.reshape(EXPERTS)


def solution(mesh):
    placed = (
        P(("ctx", "ep"), None),
        P("ctx", "ep"),
        P("ctx", "ep"),
        P("ctx", None),
        P("ctx", None),
        P(None, "ep"),
        P(None, "ep"),
        P(("ep", "ctx"), None),
        P(),
        P(),
        P("ep", None, "ctx"),
        P("ep", None, "ctx"),
        P("ep", "ctx", None),
        P(("ctx", "ep"), None),
        P(),
    )
    return jax.shard_map(
        body, mesh=mesh, in_specs=placed, out_specs=(P(("ctx", "ep"), None), P()), check_vma=False
    )
```

```python
import functools

import jax
import jax.numpy as jnp
from jax import lax
from jax.experimental import pallas as pl
from jax.experimental.pallas import tpu as pltpu
from jax.sharding import PartitionSpec as P

D = 7168
KVL = 512
NOPE = 128
ROPE = 64
VDIM = 128
HEAD_DEV = 4
SL = 896
EXPERTS = 16
META = 128
TOKENS = 64

SCORE_FLOOR = -1e30
NORM_EPS = 1e-06
ROUTE_SCALE = 2.5
LOAD_DECAY = 0.5
MESH = pl.DeviceIdType.MESH
BF = jnp.bfloat16
F32 = jnp.float32
VMEM_LIMIT = 56 * 2**20


def place():
    c = lax.axis_index("ctx")
    e = lax.axis_index("ep")
    return c, e, lax.div(c, 8), lax.rem(c, 8), lax.div(e, 2), lax.rem(e, 2)


def remote(src, dst, send, recv, device):
    return pltpu.make_async_remote_copy(
        src_ref=src, dst_ref=dst, send_sem=send, recv_sem=recv, device_id=device, device_id_type=MESH
    )


def dot(a, b):
    return jnp.dot(a, b, preferred_element_type=F32)


def dot_t(a, b):
    return lax.dot_general(a, b, (((1,), (1,)), ((), ())), preferred_element_type=F32)


def iota(shape, dim):
    return lax.broadcasted_iota(jnp.int32, shape, dim)


def selector(rows, columns, shift, width):
    row, column = iota((rows, columns), 0), iota((rows, columns), 1)
    return jnp.where((row == column + shift) & (column < width), 1.0, 0.0).astype(BF)


def column_of(block, index):
    return jnp.sum(jnp.where(iota(block.shape, 1) == index, block, 0.0), axis=1, keepdims=True)


def layer_kernel(
    q_nope, q_rope, kv, k_rope, key_up, value_up, hidden, routes, gain, ema, out_proj, router, w_gate, w_up, w_down,
    layer_out, load_out,
    KV, Q, top, total, accum, HO, WO, PB, SB, RED, RK, TS, TR, HS, HR,
    X, W, RT, ST, XC, acc0, acc1, GS, GR, A, WD, AC, DP, YB, RP, RM, SP, SM, YS, YR, OS, OR, CS, CR,
    local, kp_s, km_s, ky_s, kv_r, kf_s, kf_r, op_s, op_r, oy_s, oy_r, hd_s, hd_r,
    w_s, w_r, wf_s, wf_r, hp_s, hm_s, ho_r, sb_s, sb_r, rk_s, rk_r, t_s, t_r,
    st_s, st_r, d_s, d_r, df_s, df_r, xp_s, xm_s, xy_s, x_r, g_s, g_r, a_s, a_r,
    yb_s, yb_r, p_s, p_r, m_s, m_r, y_s, y_r, o_s, o_r, c_s, c_r,
):
    c, e, yl, z, k, s = place()
    sib = 2 * k + 1 - s
    e_half, e_row = lax.div(e, 8), lax.rem(e, 8)
    c_y = (1 - yl) * 8 + z
    sign = 1 - 2 * s

    def along(t):
        return lax.rem(z + 8 + sign * t, 8)

    c_up, c_down = yl * 8 + along(1), yl * 8 + along(-1)
    near = [along(-t) for t in range(5)]
    far = [along(t) for t in range(4)]

    def kv_rows(slot, start, size):
        return pl.ds(pl.multiple_of(slot * 128 + start, 64), size)

    def kv_slot(y, zz):
        return 2 * zz + y

    own_slot = kv_slot(yl, z)
    KV[kv_rows(own_slot, 0, 128), 0:KVL] = kv[...]
    KV[kv_rows(own_slot, 0, 128), KVL:640] = lax.dot_general(
        k_rope[...], selector(ROPE, 128, 0, ROPE), (((0,), (0,)), ((), ())),
        preferred_element_type=F32,
    ).astype(BF)

    @pl.when(yl == 0)
    def _():
        for zz in range(8):
            KV[kv_rows(kv_slot(1, zz), 0, 128), :] = jnp.zeros((128, 640), BF)

    diagonal = iota((8, 8), 0) == iota((8, 8), 1)
    route_columns = [
        jnp.sum(jnp.where(diagonal, routes[r : r + 1, :], 0), axis=1, keepdims=True)
        for r in range(2)
    ]
    route_block = jnp.where(
        iota((8, META), 1) == 0,
        route_columns[0],
        jnp.where(iota((8, META), 1) == 1, route_columns[1], 0),
    ).astype(F32)
    for kk in range(8):
        HS[kk, :, 0:SL] = hidden[:, kk * SL : (kk + 1) * SL].astype(F32)
        HS[kk, :, SL:1024] = route_block

    barrier = pltpu.get_barrier_semaphore()

    def greet(device):
        pl.semaphore_signal(barrier, 1, device_id=device, device_id_type=MESH)

    for d in range(1, 8):
        greet((yl * 8 + lax.rem(z + d, 8), e))
    greet((c_y, e))
    for d in range(1, 16):
        greet((c, lax.rem(e + d, 16)))
    turn_base = jnp.where(lax.rem(z + 8 - k, 8) < 4, 0, 4)
    turn_self = (z == k) & (k < 4)
    for q in range(4):

        @pl.when(jnp.logical_not((z == k) & (turn_base + q == k)))
        def _():
            greet((yl * 8 + k, 2 * (turn_base + q) + s))

    pl.semaphore_wait(barrier, 27 - turn_self.astype(jnp.int32))

    def kv_copy(y, zz, way):
        block = KV.at[kv_rows(kv_slot(y, zz), s * 64, 64), :]
        target = {"y": c_y, "up": c_up, "down": c_down}[way]
        sems = {"y": ky_s, "up": kp_s, "down": km_s}[way]
        slot = kv_slot(y, zz)
        return remote(block, block, sems.at[slot], kv_r.at[slot], (target, e))

    def kv_share(y, zz, core):
        slot = kv_slot(y, zz)
        block = KV.at[kv_rows(slot, core * 64, 64), :]
        return remote(block, block, kf_s.at[slot], kf_r.at[slot], (c, sib))

    kv_copy(yl, z, "up").start()
    kv_copy(yl, z, "down").start()

    @pl.when(yl == 0)
    def _():
        kv_copy(0, z, "y").start()

    def proj_copy(d):
        zz = lax.rem(z + d, 8)
        return remote(
            out_proj.at[:, pl.ds(pl.multiple_of(zz * SL, 128), SL)],
            WO.at[pl.ds(pl.multiple_of(c * 32, 32), 32), :],
            op_s.at[d],
            op_r.at[z],
            (yl * 8 + zz, e),
        )

    own_proj = pltpu.make_async_copy(
        out_proj.at[:, pl.ds(pl.multiple_of(z * SL, 128), SL)],
        WO.at[pl.ds(pl.multiple_of(c * 32, 32), 32), :],
        local.at[0],
    )
    own_proj.start()
    for d in range(1, 8):
        proj_copy(d).start()

    def hidden_copy(kk):
        return remote(
            HS.at[kk], HR.at[e_row], hd_s.at[kk], hd_r.at[e_row], (c, 2 * kk + e_half)
        )

    for kk in range(8):

        @pl.when(2 * kk + e_half != e)
        def _():
            hidden_copy(kk).start()

        @pl.when(2 * kk + e_half == e)
        def _():
            HR[e_row] = HS[kk]

    def weight_copy(d, which):
        kk = lax.rem(k + d, 8)
        source = (w_gate, w_up)[which]
        return remote(
            source.at[0, pl.ds(pl.multiple_of(kk * SL, SL), SL), :],
            W.at[e, :, pl.ds(which * 128, 128)],
            w_s.at[d, which],
            w_r.at[k, which],
            (c, 2 * kk + s),
        )

    def own_weight(which):
        source = (w_gate, w_up)[which]
        return pltpu.make_async_copy(
            source.at[0, pl.ds(pl.multiple_of(k * SL, SL), SL), :],
            W.at[e, :, pl.ds(which * 128, 128)],
            local.at[1 + which],
        )

    for which in range(2):
        own_weight(which).start()
    for d in range(1, 8):
        for which in range(2):
            weight_copy(d, which).start()
    RT[...] = jnp.zeros(RT.shape, BF)
    fetch_router = pltpu.make_async_copy(
        router.at[:, pl.ds(pl.multiple_of(k * SL, 128), SL)], RT.at[pl.ds(0, EXPERTS), :], local.at[3]
    )
    fetch_router.start()

    def down_rows(expert):
        return pl.ds(pl.multiple_of(expert * 128, 128), 128)

    def down_weight(d):
        kk = lax.rem(k + d, 8)
        return remote(
            w_down.at[0, :, pl.ds(pl.multiple_of(kk * SL, 128), SL)],
            WD.at[down_rows(e), :],
            d_s.at[d],
            d_r.at[k],
            (c, 2 * kk + s),
        )

    own_down = pltpu.make_async_copy(
        w_down.at[0, :, pl.ds(pl.multiple_of(k * SL, 128), SL)], WD.at[down_rows(e), :], local.at[4]
    )
    own_down.start()

    for h in range(HEAD_DEV):
        rows, columns = slice(h * 128, (h + 1) * 128), slice(h * 128, (h + 1) * 128)
        Q[rows, 0:KVL] = dot_t(q_nope[:, columns], key_up[:, columns]).astype(BF)
        Q[rows, KVL:640] = dot(
            q_rope[...], selector(HEAD_DEV * ROPE, 128, h * ROPE, ROPE)
        ).astype(BF)
    top[...] = jnp.full(top.shape, SCORE_FLOOR, F32)
    total[...] = jnp.zeros(total.shape, F32)
    accum[...] = jnp.zeros(accum.shape, F32)

    @pl.when(yl == 1)
    def _():
        kv_copy(0, z, "y").wait_recv()
        kv_share(0, z, s).start()

        @pl.when(s == 1)
        def _():
            kv_copy(0, z, "up").start()
            kv_copy(0, z, "down").start()

    def kv_arrive(zz, way, go_on):
        kv_copy(yl, zz, way).wait_recv()
        if go_on:
            kv_copy(yl, zz, way).start()
        kv_share(yl, zz, s).start()

        @pl.when((yl == 0) & (s == 0))
        def _():
            kv_copy(0, zz, "y").start()

        @pl.when(yl == 1)
        def _():
            kv_copy(0, zz, way).wait_recv()
            kv_share(0, zz, s).start()
            if go_on:

                @pl.when(s == 1)
                def _():
                    kv_copy(0, zz, way).start()

    score_scale = (NOPE + ROPE) ** (-0.5)

    def attend(zz, own):
        if not own:
            kv_share(yl, zz, 1 - s).wait_recv()

        @pl.when(yl == 1)
        def _():
            kv_share(0, zz, 1 - s).wait_recv()

        @pl.when((yl == 1) | (zz <= z))
        def _():
            keys = KV[pl.ds(pl.multiple_of(zz * 256, 256), 256), :]
            scores = dot_t(Q[...], keys)
            query_pos = c * 128 + (iota(scores.shape, 0) & 127)
            column = iota(scores.shape, 1)
            key_pos = zz * 128 + jnp.where(column < 128, column, column + (1024 - 128))
            scores = jnp.where(key_pos <= query_pos, scores, SCORE_FLOOR)
            top_old = top[...]
            top_new = jnp.maximum(top_old, jnp.max(scores, axis=1, keepdims=True))
            exp_scores = jnp.exp((scores - top_new) * score_scale)
            shrink = jnp.exp((top_old - top_new) * score_scale)
            top[...] = top_new
            total[...] = total[...] * shrink + jnp.sum(exp_scores, axis=1, keepdims=True)
            accum[...] = accum[...] * shrink + dot(exp_scores.astype(BF), keys[:, 0:KVL])

    def proj_piece(zz):
        piece = WO.at[pl.ds(pl.multiple_of((yl * 8 + zz) * 32, 32), 32), :]
        return remote(out_proj.at[:, pl.ds(0, SL)], piece, op_s.at[0], op_r.at[zz], (c, e))

    def proj_share(y):
        row = WO.at[pl.ds(pl.multiple_of(y * 256, 256), 256), :]
        return remote(row, row, oy_s.at[0], oy_r.at[0], (c_y, e))

    kv_arrive(near[1], "up", True)
    kv_arrive(far[1], "down", True)
    attend(z, True)
    kv_arrive(near[2], "up", True)
    kv_arrive(far[2], "down", True)
    attend(near[1], False)
    attend(far[1], False)
    kv_arrive(near[3], "up", True)
    kv_arrive(far[3], "down", False)
    attend(near[2], False)
    attend(far[2], False)
    kv_arrive(near[4], "up", False)
    own_proj.wait()
    for d in range(1, 8):
        proj_piece(lax.rem(z + d, 8)).wait_recv()
    proj_share(yl).start()
    attend(near[3], False)
    attend(far[3], False)
    attend(near[4], False)

    own_rows = pl.ds(pl.multiple_of(z * 128, 128), 128)
    for h in range(HEAD_DEV):
        rows, columns = slice(h * 128, (h + 1) * 128), slice(h * 128, (h + 1) * 128)
        latent = (accum[rows, :] / total[rows, :]).astype(BF)
        HO[own_rows, columns] = dot(latent, value_up[:, columns]).astype(BF)

    def ho_copy(zz, half, up):
        block = HO.at[pl.ds(pl.multiple_of(zz * 128 + half * 64, 64), 64), :]
        target = yl * 8 + lax.rem(z + (1 if up else 7), 8)
        return remote(
            block, block, (hp_s if up else hm_s).at[zz, half], ho_r.at[zz, half], (target, e)
        )

    for half in range(2):
        ho_copy(z, half, True).start()
        ho_copy(z, half, False).start()
    proj_share(1 - yl).wait_recv()

    def ho_arrive(zz, up, go_on):
        for half in range(2):
            ho_copy(zz, half, up).wait_recv()
            if go_on:
                ho_copy(zz, half, up).start()

    def sib_copy(zz):
        return remote(
            PB.at[zz, pl.ds(pl.multiple_of((1 - s) * 64, 64), 64), :],
            SB.at[zz],
            sb_s.at[zz],
            sb_r.at[zz],
            (c, sib),
        )

    below = [lax.rem(z + 8 - t, 8) for t in range(5)]
    above = [lax.rem(z + t, 8) for t in range(4)]
    ho_pairs = [(z, below[1])] + [(above[t], below[t + 1]) for t in range(1, 4)]

    def project(t):
        for zz in ho_pairs[t]:
            PB[zz] = dot(HO[pl.ds(pl.multiple_of(zz * 128, 128), 128), :], WO[...]).astype(BF)
            sib_copy(zz).start()

    def rows16(index):
        return pl.ds(pl.multiple_of(index * 16, 16), 16)

    def chip_copy(t, d):
        kk = lax.rem(k + d, 8)
        return remote(
            RED.at[t, rows16(kk), :], RK.at[t, k], rk_s.at[t, d], rk_r.at[t, k], (c, 2 * kk + s)
        )

    def reduce_cores(t):
        for i, zz in enumerate(ho_pairs[t]):
            sib_copy(zz).wait_recv()
            own = PB[zz, pl.ds(pl.multiple_of(s * 64, 64), 64), :]
            RED[t, i * 64 : (i + 1) * 64, :] = (own.astype(F32) + SB[zz].astype(F32)).astype(BF)
        for d in range(1, 8):
            chip_copy(t, d).start()
        RK[t, k] = RED[t, rows16(k), :]

    quarter = lax.rem(k, 4)

    def turn_copy(t):
        za, zb = ho_pairs[t]
        target = jnp.where(k < 4, za, zb)
        return remote(
            TS.at[t], TR.at[rows16(quarter), :], t_s.at[t], t_r.at[quarter],
            (yl * 8 + target, 2 * z + s),
        )

    def reduce_chips(t):
        for d in range(1, 8):
            kk = lax.rem(k + d, 8)
            remote(TS.at[t], RK.at[t, kk], t_s.at[0], rk_r.at[t, kk], (c, e)).wait_recv()
        summed = RK[t, 0].astype(F32)
        for kk in range(1, 8):
            summed = summed + RK[t, kk].astype(F32)
        TS[t] = summed.astype(BF)
        if t > 0:
            turn_copy(t).start()
            return

        @pl.when(turn_self)
        def _():
            TR[rows16(quarter), :] = TS[t]

        @pl.when(jnp.logical_not(turn_self))
        def _():
            turn_copy(t).start()

    ho_arrive(below[1], True, True)
    project(0)
    ho_arrive(above[1], False, True)
    ho_arrive(below[2], True, True)
    project(1)
    reduce_cores(0)
    ho_arrive(above[2], False, True)
    ho_arrive(below[3], True, True)
    project(2)
    reduce_cores(1)
    reduce_chips(0)
    ho_arrive(above[3], False, False)
    ho_arrive(below[4], True, False)
    project(3)
    reduce_cores(2)
    reduce_chips(1)
    reduce_cores(3)
    reduce_chips(2)

    for which in range(2):
        own_weight(which).wait()

    def weight_share(kk, core):
        expert = 2 * kk + core
        return remote(W.at[expert], W.at[expert], wf_s.at[kk], wf_r.at[kk], (c, sib))

    def share_weights():
        weight_share(k, s).start()
        for d in range(1, 8):
            kk = lax.rem(k + d, 8)
            for which in range(2):
                piece = W.at[2 * kk + s, :, pl.ds(which * 128, 128)]
                remote(piece, piece, w_s.at[0, which], w_r.at[kk, which], (c, e)).wait_recv()
            weight_share(kk, s).start()

    reduce_chips(3)
    for d in range(1, 8):
        down_weight(d).start()

    for j in range(8):

        @pl.when(8 * s + j != e)
        def _():
            remote(HS.at[0], HR.at[j], hd_s.at[0], hd_r.at[j], (c, e)).wait_recv()

    fetch_router.wait()
    for q in range(4):

        @pl.when(jnp.logical_not((z == k) & (turn_base + q == k)))
        def _():
            remote(TS.at[0], TR.at[rows16(q), :], t_s.at[0], t_r.at[q], (c, e)).wait_recv()

    rows_in = HR[...].reshape(TOKENS, 1024)
    residual = (rows_in[:, 0:SL] + TR[...].astype(F32)).astype(BF).astype(F32)
    gains = gain[k]
    lane = iota((TOKENS, META), 1)
    logits = dot_t((residual * gains).astype(BF), RT[...])
    squares = jnp.sum(residual * residual, axis=1, keepdims=True)
    ST[k] = jnp.where(lane == EXPERTS, squares, logits)

    def stat_copy(d):
        kk = lax.rem(k + d, 8)
        return remote(ST.at[k], ST.at[k], st_s.at[d], st_r.at[k], (c, 2 * kk + s))

    for d in range(1, 8):
        stat_copy(d).start()
    for d in range(1, 8):
        kk = lax.rem(k + d, 8)
        remote(ST.at[kk], ST.at[kk], st_s.at[0], st_r.at[kk], (c, e)).wait_recv()
    stats = ST[0]
    for kk in range(1, 8):
        stats = stats + ST[kk]
    inverse = lax.rsqrt(column_of(stats, EXPERTS) / D + NORM_EPS)
    normed = (residual * inverse * gains).astype(BF)
    affinity = 1.0 / (1.0 + jnp.exp(-(stats * inverse)))
    routed = rows_in[:, SL:1024]
    route0, route1 = column_of(routed, 0), column_of(routed, 1)
    lane_f = lane.astype(F32)
    chosen0 = jnp.sum(jnp.where(lane_f == route0, affinity, 0.0), axis=1, keepdims=True)
    chosen1 = jnp.sum(jnp.where(lane_f == route1, affinity, 0.0), axis=1, keepdims=True)
    scale = ROUTE_SCALE / (chosen0 + chosen1)
    meta = jnp.where(lane == 0, route0, jnp.where(lane == 1, route1, 0.0))
    for index, weight in ((2, chosen0 * scale), (4, chosen1 * scale)):
        coarse = weight.astype(BF).astype(F32)
        meta = jnp.where(lane == index, coarse, meta)
        meta = jnp.where(lane == index + 1, weight - coarse, meta)

    def rows_of(cc):
        return pl.ds(pl.multiple_of(cc * TOKENS, TOKENS), TOKENS)

    X[rows_of(c), 0:SL] = normed
    X[rows_of(c), SL:1024] = meta.astype(BF)

    def row_copy(cc, way):
        block = X.at[rows_of(cc), :]
        target = {"y": c_y, "up": c_up, "down": c_down}[way]
        sems = {"y": xy_s, "up": xp_s, "down": xm_s}[way]
        return remote(block, block, sems.at[cc], x_r.at[cc], (target, e))

    row_copy(c, "up").start()
    row_copy(c, "down").start()
    row_copy(c, "y").start()
    row_copy(c_y, "y").wait_recv()

    @pl.when(s == 0)
    def _():
        row_copy(c_y, "up").start()
        row_copy(c_y, "down").start()

    def arrive(zz, way, go_on):
        own, other = yl * 8 + zz, (1 - yl) * 8 + zz
        row_copy(own, way).wait_recv()
        if go_on:
            row_copy(own, way).start()

        @pl.when(s == 1)
        def _():
            row_copy(own, "y").start()

        row_copy(other, way).wait_recv()
        if go_on:

            @pl.when(s == 0)
            def _():
                row_copy(other, way).start()

    chunks = [(z, near[1])] + [(far[t], near[t + 1]) for t in range(1, 4)]

    def places(t):
        za, zb = chunks[t]
        return [(0, za), (1, za), (0, zb), (1, zb)]

    def part(kk):
        return pl.ds(pl.multiple_of(kk * 32, 32), 32)

    def half_copy(t, d):
        kk = lax.rem(k + d, 8)
        return remote(
            GS.at[t, :, part(kk), :], GR.at[t, k], g_s.at[t, d], g_r.at[t, k], (c, 2 * kk + s)
        )

    def first_layers(t):
        for i, (y, zz) in enumerate(places(t)):
            XC[t, i * 64 : (i + 1) * 64, :] = X[rows_of(y * 8 + zz), :]
        acc0[...] = jnp.zeros(acc0.shape, F32)
        acc1[...] = jnp.zeros(acc1.shape, F32)
        routed_here = XC[t, :, SL:1024].astype(F32)
        r0, r1 = column_of(routed_here, 0), column_of(routed_here, 1)

        def one_expert(expert, carry):
            product = dot(XC[t, :, 0:SL], W[expert])
            number = expert.astype(F32)
            acc0[...] += jnp.where(r0 == number, product, 0.0)
            acc1[...] += jnp.where(r1 == number, product, 0.0)
            return carry

        lax.fori_loop(0, EXPERTS, one_expert, 0)
        GS[t, 0] = acc0[...].astype(BF)
        GS[t, 1] = acc1[...].astype(BF)
        for d in range(1, 8):
            half_copy(t, d).start()
        GR[t, k] = GS[t, :, part(k), :]

    def act_copy(t, d):
        kk = lax.rem(k + d, 8)
        block = A.at[t, :, part(k), :]
        return remote(block, block, a_s.at[t, d], a_r.at[t, k], (c, 2 * kk + s))

    def activate(t):
        for d in range(1, 8):
            kk = lax.rem(k + d, 8)
            remote(GR.at[t, k], GR.at[t, kk], g_s.at[t, 0], g_r.at[t, kk], (c, e)).wait_recv()
        here = XC[t, part(k), SL:1024].astype(F32)
        for r in range(2):
            both = GR[t, 0, r].astype(F32)
            for kk in range(1, 8):
                both = both + GR[t, kk, r].astype(F32)
            weight = column_of(here, 2 + 2 * r) + column_of(here, 3 + 2 * r)
            gate, up = both[:, 0:128], both[:, 128:256]
            A[t, r, part(k), :] = (gate / (1.0 + jnp.exp(-gate)) * up * weight).astype(BF)
        for d in range(1, 8):
            act_copy(t, d).start()

    def partner_copy(y, zz):
        return remote(DP.at[zz, y], YB.at[zz], yb_s.at[zz], yb_r.at[zz], (c_y, e))

    def second_layer(t):
        for d in range(1, 8):
            kk = lax.rem(k + d, 8)
            block = A.at[t, :, part(kk), :]
            remote(block, block, a_s.at[t, 0], a_r.at[t, kk], (c, e)).wait_recv()
        routed_here = XC[t, :, SL:1024].astype(F32)
        r0, r1 = column_of(routed_here, 0), column_of(routed_here, 1)
        a0, a1 = A[t, 0].astype(F32), A[t, 1].astype(F32)
        for expert in range(EXPERTS):
            picked = jnp.where(r0 == float(expert), a0, 0.0) + jnp.where(
                r1 == float(expert), a1, 0.0
            )
            AC[:, expert * 128 : (expert + 1) * 128] = picked.astype(BF)
        out = dot(AC[...], WD[...])
        for i, (y, zz) in enumerate(places(t)):
            DP[zz, y] = out[i * 64 : (i + 1) * 64, :].astype(BF)

        @pl.when(s == 1)
        def _():
            for zz in chunks[t]:
                partner_copy(1 - yl, zz).start()

    def down_share(kk, core):
        block = WD.at[down_rows(2 * kk + core), :]
        return remote(block, block, df_s.at[kk], df_r.at[kk], (c, sib))

    arrive(near[1], "up", True)
    arrive(far[1], "down", True)
    share_weights()
    arrive(near[2], "up", True)
    arrive(far[2], "down", True)
    for kk in range(8):
        weight_share(kk, 1 - s).wait_recv()
    first_layers(0)
    arrive(near[3], "up", True)
    arrive(far[3], "down", False)
    first_layers(1)
    arrive(near[4], "up", False)
    activate(0)
    first_layers(2)
    activate(1)
    own_down.wait()
    down_share(k, s).start()
    for d in range(1, 8):
        kk = lax.rem(k + d, 8)
        block = WD.at[down_rows(2 * kk + s), :]
        remote(block, block, d_s.at[0], d_r.at[kk], (c, e)).wait_recv()
        down_share(kk, s).start()
    first_layers(3)
    activate(2)
    for kk in range(8):
        down_share(kk, 1 - s).wait_recv()
    second_layer(0)
    second_layer(1)
    activate(3)

    routed_all = X[:, SL:1024].astype(F32)
    lane_all = iota(routed_all.shape, 1).astype(F32)
    named = jnp.where(lane_all == column_of(routed_all, 0), 1.0, 0.0) + jnp.where(
        lane_all == column_of(routed_all, 1), 1.0, 0.0
    )
    CS[...] = jnp.broadcast_to(jnp.sum(named, axis=0, keepdims=True), CS.shape)
    count_copy = remote(CS, CR, c_s.at[0], c_r.at[0], (c, sib))
    count_copy.start()

    second_layer(2)
    second_layer(3)

    def joins(y):
        return (s == 0) | (y == yl)

    def complete(zz):
        @pl.when(s == 1)
        def _():
            partner_copy(yl, zz).wait_recv()
            DP[zz, yl] = (DP[zz, yl].astype(F32) + YB[zz].astype(F32)).astype(BF)

    def up_copy(source, step, y):
        return remote(source, RP.at[step, y], p_s.at[step, y], p_r.at[step, y], (c_up, e))

    def down_copy(source, step, y):
        return remote(source, RM.at[step, y], m_s.at[step, y], m_r.at[step, y], (c_down, e))

    ups = [along(4 - t) for t in range(5)]
    downs = [along(t - 3) for t in range(4)]
    complete(ups[0])
    complete(downs[0])
    for y in range(2):

        @pl.when(joins(y))
        def _():
            up_copy(DP.at[ups[0], y], 0, y).start()
            down_copy(DP.at[downs[0], y], 0, y).start()

    for t in range(1, 4):
        complete(ups[t])
        complete(downs[t])
        for y in range(2):

            @pl.when(joins(y))
            def _():
                up_copy(SP.at[0, y], t - 1, y).wait_recv()
                SP[t - 1, y] = (
                    DP[ups[t], y].astype(F32) + RP[t - 1, y].astype(F32)
                ).astype(BF)
                up_copy(SP.at[t - 1, y], t, y).start()
                if t < 3:
                    down_copy(SM.at[0, y], t - 1, y).wait_recv()
                    SM[t - 1, y] = (
                        DP[downs[t], y].astype(F32) + RM[t - 1, y].astype(F32)
                    ).astype(BF)
                    down_copy(SM.at[t - 1, y], t, y).start()

    def final(y):
        down_copy(SM.at[0, 0], 2, y).wait_recv()
        up_copy(SP.at[0, 0], 3, y).wait_recv()
        return DP[z, y].astype(F32) + RP[3, y].astype(F32) + RM[2, y].astype(F32)

    y_copy = remote(YS, YR, y_s.at[0], y_r.at[0], (c_y, e))

    @pl.when(s == 0)
    def _():
        YS[...] = final(1 - yl).astype(BF)
        y_copy.start()

    OS[...] = final(yl) + residual

    @pl.when(s == 0)
    def _():
        y_copy.wait_recv()
        OS[...] += YR[...].astype(F32)

    def owner_copy(j):
        return remote(
            OS.at[pl.ds(j * 8, 8), :], OR.at[k], o_s.at[j], o_r.at[k], (c, 8 * s + j)
        )

    for j in range(8):

        @pl.when(8 * s + j != e)
        def _():
            owner_copy(j).start()

        @pl.when(8 * s + j == e)
        def _():
            OR[k] = OS[pl.ds(j * 8, 8), :]

    count_copy.wait_recv()
    counts = (CS[...] + CR[...])[0:1, 0:EXPERTS]
    load_out[...] = LOAD_DECAY * ema[...] + (1.0 - LOAD_DECAY) * counts / 256.0

    for zz in range(8):
        sib_copy(zz).wait_send()
        weight_share(zz, s).wait_send()
        down_share(zz, s).wait_send()

        @pl.when(2 * zz + e_half != e)
        def _():
            hidden_copy(zz).wait_send()

        @pl.when(s == 1)
        def _():
            partner_copy(1 - yl, zz).wait_send()

    for d in range(1, 8):
        proj_copy(d).wait_send()
        down_weight(d).wait_send()
        stat_copy(d).wait_send()
        for which in range(2):
            weight_copy(d, which).wait_send()
        for t in range(4):
            chip_copy(t, d).wait_send()
            half_copy(t, d).wait_send()
            act_copy(t, d).wait_send()
    proj_share(yl).wait_send()

    @pl.when(jnp.logical_not(turn_self))
    def _():
        turn_copy(0).wait_send()

    for t in range(1, 4):
        turn_copy(t).wait_send()
    for half in range(2):
        for t in range(4):
            ho_copy(below[t], half, True).wait_send()
        for t in range(3):
            ho_copy(above[t], half, False).wait_send()

    both_rows = (yl == 1) & (s == 1)
    for t in range(8):
        zz = lax.rem(z + t, 8)
        if t > 0:
            kv_share(yl, zz, s).wait_send()

        @pl.when(yl == 1)
        def _():
            kv_share(0, zz, s).wait_send()

        @pl.when((yl == 0) & ((s == 0) | (zz == z)))
        def _():
            kv_copy(0, zz, "y").wait_send()

        @pl.when((s == 1) | (zz == z))
        def _():
            row_copy(yl * 8 + zz, "y").wait_send()

    for t in range(4):
        kv_copy(yl, near[t], "up").wait_send()
        row_copy(yl * 8 + near[t], "up").wait_send()

        @pl.when(both_rows)
        def _():
            kv_copy(0, near[t], "up").wait_send()

        @pl.when(s == 0)
        def _():
            row_copy((1 - yl) * 8 + near[t], "up").wait_send()

    for t in range(3):
        kv_copy(yl, far[t], "down").wait_send()
        row_copy(yl * 8 + far[t], "down").wait_send()

        @pl.when(both_rows)
        def _():
            kv_copy(0, far[t], "down").wait_send()

        @pl.when(s == 0)
        def _():
            row_copy((1 - yl) * 8 + far[t], "down").wait_send()

    for y in range(2):

        @pl.when(joins(y))
        def _():
            up_copy(DP.at[ups[0], y], 0, y).wait_send()
            down_copy(DP.at[downs[0], y], 0, y).wait_send()
            for t in range(1, 4):
                up_copy(SP.at[t - 1, y], t, y).wait_send()
                if t < 3:
                    down_copy(SM.at[t - 1, y], t, y).wait_send()

    @pl.when(s == 0)
    def _():
        y_copy.wait_send()

    count_copy.wait_send()
    for j in range(8):

        @pl.when(8 * s + j != e)
        def _():
            owner_copy(j).wait_send()

    for kk in range(8):

        @pl.when(2 * kk + e_half != e)
        def _():
            remote(
                OS.at[pl.ds(0, 8), :], OR.at[kk], o_s.at[0], o_r.at[kk], (c, e)
            ).wait_recv()

        layer_out[:, kk * SL : (kk + 1) * SL] = OR[kk].astype(BF)


def in_vmem(count):
    return [pl.BlockSpec(memory_space=pltpu.VMEM)] * count


def anywhere(count):
    return [pl.BlockSpec(memory_space=pl.ANY)] * count


def dma(*shape):
    return pltpu.SemaphoreType.DMA(shape)


def shaped(shape, dtype):
    return jax.ShapeDtypeStruct(shape, dtype)


def params(number):
    return pltpu.CompilerParams(
        collective_id=number, has_side_effects=True, vmem_limit_bytes=VMEM_LIMIT
    )


def body(
    hidden, q_nope, q_rope, kv_latent, k_rope, key_up, value_up, out_proj, ffn_gain, router,
    w_gate, w_up, w_down, routes, load_ema,
):
    v = pltpu.VMEM
    layer_out, new_load = pl.pallas_call(
        layer_kernel,
        out_shape=(shaped((8, D), BF), shaped((1, EXPERTS), F32)),
        in_specs=in_vmem(10) + anywhere(5),
        out_specs=tuple(in_vmem(2)),
        scratch_shapes=[
            v((2048, 640), BF), v((512, 640), BF), v((512, 1), F32), v((512, 1), F32),
            v((512, 512), F32), v((1024, 512), BF), v((512, SL), BF), v((8, 128, SL), BF),
            v((8, 64, SL), BF), v((4, 128, SL), BF), v((4, 8, 16, SL), BF), v((4, 16, SL), BF),
            v((64, SL), BF), v((8, 8, 1024), F32), v((8, 8, 1024), F32),
            v((1024, 1024), BF), v((16, SL, 256), BF), v((128, SL), BF), v((8, 64, META), F32),
            v((4, 256, 1024), BF), v((256, 256), F32), v((256, 256), F32),
            v((4, 2, 256, 256), BF), v((4, 8, 2, 32, 256), BF), v((4, 2, 256, 128), BF),
            v((2048, SL), BF), v((256, 2048), BF), v((8, 2, 64, SL), BF), v((8, 64, SL), BF),
            v((4, 2, 64, SL), BF), v((3, 2, 64, SL), BF), v((3, 2, 64, SL), BF),
            v((2, 2, 64, SL), BF), v((64, SL), BF), v((64, SL), BF), v((64, SL), F32),
            v((8, 8, SL), F32), v((8, 128), F32), v((8, 128), F32),
            dma(5), dma(16), dma(16), dma(16), dma(16), dma(16), dma(16), dma(8), dma(8),
            dma(1), dma(1), dma(8), dma(8),
            dma(8, 2), dma(8, 2), dma(8), dma(8), dma(8, 2), dma(8, 2), dma(8, 2), dma(8), dma(8),
            dma(4, 8), dma(4, 8), dma(4), dma(4),
            dma(8), dma(8), dma(8), dma(8), dma(8), dma(8), dma(16), dma(16), dma(16), dma(16),
            dma(4, 8), dma(4, 8), dma(4, 8), dma(4, 8),
            dma(8), dma(8), dma(4, 2), dma(4, 2), dma(3, 2), dma(3, 2), dma(1), dma(1), dma(8),
            dma(8), dma(1), dma(1),
        ],
        compiler_params=params(0),
        name="layer",
    )(
        q_nope, q_rope, kv_latent, k_rope.T, key_up, value_up, hidden, routes.T,
        ffn_gain.reshape(8, 1, SL), load_ema.reshape(1, EXPERTS), out_proj, router.T, w_gate, w_up, w_down,
    )
    return layer_out, new_load.reshape(EXPERTS)


def solution(mesh):
    placed = (
        P(("ctx", "ep"), None),
        P("ctx", "ep"),
        P("ctx", "ep"),
        P("ctx", None),
        P("ctx", None),
        P(None, "ep"),
        P(None, "ep"),
        P(("ep", "ctx"), None),
        P(),
        P(),
        P("ep", None, "ctx"),
        P("ep", None, "ctx"),
        P("ep", "ctx", None),
        P(("ctx", "ep"), None),
        P(),
    )
    return jax.shard_map(
        body, mesh=mesh, in_specs=placed, out_specs=(P(("ctx", "ep"), None), P()), check_vma=False
    )
```

```python
import functools

import jax
import jax.numpy as jnp
from jax import lax
from jax.experimental import pallas as pl
from jax.experimental.pallas import tpu as pltpu
from jax.sharding import PartitionSpec as P

D = 7168
KVL = 512
NOPE = 128
ROPE = 64
VDIM = 128
HEAD_DEV = 4
SL = 896
EXPERTS = 16
META = 128
TOKENS = 64

SCORE_FLOOR = -1e30
NORM_EPS = 1e-06
ROUTE_SCALE = 2.5
LOAD_DECAY = 0.5
MESH = pl.DeviceIdType.MESH
BF = jnp.bfloat16
F32 = jnp.float32
VMEM_LIMIT = 56 * 2**20


def place():
    c = lax.axis_index("ctx")
    e = lax.axis_index("ep")
    return c, e, lax.div(c, 8), lax.rem(c, 8), lax.div(e, 2), lax.rem(e, 2)


def remote(src, dst, send, recv, device):
    return pltpu.make_async_remote_copy(
        src_ref=src, dst_ref=dst, send_sem=send, recv_sem=recv, device_id=device, device_id_type=MESH
    )


def dot(a, b):
    return jnp.dot(a, b, preferred_element_type=F32)


def dot_t(a, b):
    return lax.dot_general(a, b, (((1,), (1,)), ((), ())), preferred_element_type=F32)


def iota(shape, dim):
    return lax.broadcasted_iota(jnp.int32, shape, dim)


def selector(rows, columns, shift, width):
    row, column = iota((rows, columns), 0), iota((rows, columns), 1)
    return jnp.where((row == column + shift) & (column < width), 1.0, 0.0).astype(BF)


def column_of(block, index):
    return jnp.sum(jnp.where(iota(block.shape, 1) == index, block, 0.0), axis=1, keepdims=True)


def layer_kernel(
    q_nope, q_rope, kv, k_rope, key_up, value_up, hidden, routes, gain, ema, out_proj, router, w_gate, w_up, w_down,
    layer_out, load_out,
    KV, Q, top, total, accum, HO, WO, PB, SB, RED, RK, TS, TR, HS, HR,
    X, W, RT, ST, XC, acc0, acc1, GS, GR, A, WD, AC, DP, YB, RP, RM, SP, SM, YS, YR, OS, OR, CS, CR, MS, MR,
    local, kp_s, km_s, ky_s, kv_r, kf_s, kf_r, op_s, op_r, oy_s, oy_r, hd_s, hd_r,
    w_s, w_r, wf_s, wf_r, hp_s, hm_s, ho_r, sb_s, sb_r, rk_s, rk_r, t_s, t_r,
    st_s, st_r, d_s, d_r, df_s, df_r, xp_s, xm_s, xy_s, x_r, g_s, g_r, a_s, a_r,
    yb_s, yb_r, p_s, p_r, m_s, m_r, y_s, y_r, o_s, o_r, c_s, c_r, ms_s, ms_r,
):
    c, e, yl, z, k, s = place()
    sib = 2 * k + 1 - s
    e_half, e_row = lax.div(e, 8), lax.rem(e, 8)
    c_y = (1 - yl) * 8 + z
    sign = 1 - 2 * s

    def along(t):
        return lax.rem(z + 8 + sign * t, 8)

    c_up, c_down = yl * 8 + along(1), yl * 8 + along(-1)
    near = [along(-t) for t in range(5)]
    far = [along(t) for t in range(4)]

    def kv_rows(slot, start, size):
        return pl.ds(pl.multiple_of(slot * 128 + start, 64), size)

    def kv_slot(y, zz):
        return 2 * zz + y

    own_slot = kv_slot(yl, z)
    KV[kv_rows(own_slot, 0, 128), 0:KVL] = kv[...]
    KV[kv_rows(own_slot, 0, 128), KVL:640] = lax.dot_general(
        k_rope[...], selector(ROPE, 128, 0, ROPE), (((0,), (0,)), ((), ())),
        preferred_element_type=F32,
    ).astype(BF)

    @pl.when(yl == 0)
    def _():
        for zz in range(8):
            KV[kv_rows(kv_slot(1, zz), 0, 128), :] = jnp.zeros((128, 640), BF)

    diagonal = iota((8, 8), 0) == iota((8, 8), 1)
    route_columns = [
        jnp.sum(jnp.where(diagonal, routes[r : r + 1, :], 0), axis=1, keepdims=True)
        for r in range(2)
    ]
    route_block = jnp.where(
        iota((8, META), 1) == 0,
        route_columns[0],
        jnp.where(iota((8, META), 1) == 1, route_columns[1], 0),
    ).astype(F32)
    for kk in range(8):
        HS[kk, :, 0:SL] = hidden[:, kk * SL : (kk + 1) * SL].astype(F32)
        HS[kk, :, SL:1024] = route_block

    barrier = pltpu.get_barrier_semaphore()

    def greet(device):
        pl.semaphore_signal(barrier, 1, device_id=device, device_id_type=MESH)

    for d in range(1, 8):
        greet((yl * 8 + lax.rem(z + d, 8), e))
    greet((c_y, e))
    for d in range(1, 16):
        greet((c, lax.rem(e + d, 16)))
    turn_base = jnp.where(lax.rem(z + 8 - k, 8) < 4, 0, 4)
    turn_self = (z == k) & (k < 4)
    for q in range(4):

        @pl.when(jnp.logical_not((z == k) & (turn_base + q == k)))
        def _():
            greet((yl * 8 + k, 2 * (turn_base + q) + s))

    scale_row = lax.rem(lax.div(k, 2), 2)

    def scale_source(t):
        return scale_row * 8 + jnp.where(k < 4, along(t), along(-1 - t))

    for t in range(4):

        @pl.when(scale_source(t) != c)
        def _():
            greet((scale_source(t), e))

    scale_sends = jnp.where(yl == scale_row, jnp.where(k < 4, 7, 8), 0)
    pl.semaphore_wait(barrier, 27 - turn_self.astype(jnp.int32) + scale_sends)

    def kv_copy(y, zz, way):
        block = KV.at[kv_rows(kv_slot(y, zz), s * 64, 64), :]
        target = {"y": c_y, "up": c_up, "down": c_down}[way]
        sems = {"y": ky_s, "up": kp_s, "down": km_s}[way]
        slot = kv_slot(y, zz)
        return remote(block, block, sems.at[slot], kv_r.at[slot], (target, e))

    def kv_share(y, zz, core):
        slot = kv_slot(y, zz)
        block = KV.at[kv_rows(slot, core * 64, 64), :]
        return remote(block, block, kf_s.at[slot], kf_r.at[slot], (c, sib))

    kv_copy(yl, z, "up").start()
    kv_copy(yl, z, "down").start()

    @pl.when(yl == 0)
    def _():
        kv_copy(0, z, "y").start()

    def proj_copy(d):
        zz = lax.rem(z + d, 8)
        return remote(
            out_proj.at[:, pl.ds(pl.multiple_of(zz * SL, 128), SL)],
            WO.at[pl.ds(pl.multiple_of(c * 32, 32), 32), :],
            op_s.at[d],
            op_r.at[z],
            (yl * 8 + zz, e),
        )

    own_proj = pltpu.make_async_copy(
        out_proj.at[:, pl.ds(pl.multiple_of(z * SL, 128), SL)],
        WO.at[pl.ds(pl.multiple_of(c * 32, 32), 32), :],
        local.at[0],
    )
    own_proj.start()
    for d in range(1, 8):
        proj_copy(d).start()

    def hidden_copy(kk):
        return remote(
            HS.at[kk], HR.at[e_row], hd_s.at[kk], hd_r.at[e_row], (c, 2 * kk + e_half)
        )

    for kk in range(8):

        @pl.when(2 * kk + e_half != e)
        def _():
            hidden_copy(kk).start()

        @pl.when(2 * kk + e_half == e)
        def _():
            HR[e_row] = HS[kk]

    def weight_copy(d, which):
        kk = lax.rem(k + d, 8)
        source = (w_gate, w_up)[which]
        return remote(
            source.at[0, pl.ds(pl.multiple_of(kk * SL, SL), SL), :],
            W.at[e, :, pl.ds(which * 128, 128)],
            w_s.at[d, which],
            w_r.at[k, which],
            (c, 2 * kk + s),
        )

    def own_weight(which):
        source = (w_gate, w_up)[which]
        return pltpu.make_async_copy(
            source.at[0, pl.ds(pl.multiple_of(k * SL, SL), SL), :],
            W.at[e, :, pl.ds(which * 128, 128)],
            local.at[1 + which],
        )

    for which in range(2):
        own_weight(which).start()
    for d in range(1, 8):
        for which in range(2):
            weight_copy(d, which).start()
    RT[...] = jnp.zeros(RT.shape, BF)
    fetch_router = pltpu.make_async_copy(
        router.at[:, pl.ds(pl.multiple_of(k * SL, 128), SL)], RT.at[pl.ds(0, EXPERTS), :], local.at[3]
    )
    fetch_router.start()

    def down_rows(expert):
        return pl.ds(pl.multiple_of(expert * 128, 128), 128)

    def down_weight(d):
        kk = lax.rem(k + d, 8)
        return remote(
            w_down.at[0, :, pl.ds(pl.multiple_of(kk * SL, 128), SL)],
            WD.at[down_rows(e), :],
            d_s.at[d],
            d_r.at[k],
            (c, 2 * kk + s),
        )

    own_down = pltpu.make_async_copy(
        w_down.at[0, :, pl.ds(pl.multiple_of(k * SL, 128), SL)], WD.at[down_rows(e), :], local.at[4]
    )
    own_down.start()

    for h in range(HEAD_DEV):
        rows, columns = slice(h * 128, (h + 1) * 128), slice(h * 128, (h + 1) * 128)
        Q[rows, 0:KVL] = dot_t(q_nope[:, columns], key_up[:, columns]).astype(BF)
        Q[rows, KVL:640] = dot(
            q_rope[...], selector(HEAD_DEV * ROPE, 128, h * ROPE, ROPE)
        ).astype(BF)
    top[...] = jnp.full(top.shape, SCORE_FLOOR, F32)
    total[...] = jnp.zeros(total.shape, F32)
    accum[...] = jnp.zeros(accum.shape, F32)

    @pl.when(yl == 1)
    def _():
        kv_copy(0, z, "y").wait_recv()
        kv_share(0, z, s).start()

        kv_copy(0, z, "up").start()
        kv_copy(0, z, "down").start()

    def kv_arrive(zz, way, go_on):
        kv_copy(yl, zz, way).wait_recv()

        @pl.when(go_on)
        def _():
            kv_copy(yl, zz, way).start()

        kv_share(yl, zz, s).start()

        @pl.when(yl == 1)
        def _():
            kv_copy(0, zz, way).wait_recv()
            kv_share(0, zz, s).start()

            @pl.when(go_on)
            def _():
                kv_copy(0, zz, way).start()

    score_scale = (NOPE + ROPE) ** (-0.5)

    def attend(zz, shared):
        @pl.when(shared)
        def _():
            kv_share(yl, zz, 1 - s).wait_recv()

        @pl.when(yl == 1)
        def _():
            kv_share(0, zz, 1 - s).wait_recv()

        @pl.when((yl == 1) | (zz <= z))
        def _():
            keys = KV[pl.ds(pl.multiple_of(zz * 256, 256), 256), :]
            scores = dot_t(Q[...], keys)
            query_pos = c * 128 + (iota(scores.shape, 0) & 127)
            column = iota(scores.shape, 1)
            key_pos = zz * 128 + jnp.where(column < 128, column, column + (1024 - 128))
            scores = jnp.where(key_pos <= query_pos, scores, SCORE_FLOOR)
            top_old = top[...]
            top_new = jnp.maximum(top_old, jnp.max(scores, axis=1, keepdims=True))
            exp_scores = jnp.exp((scores - top_new) * score_scale)
            shrink = jnp.exp((top_old - top_new) * score_scale)
            top[...] = top_new
            total[...] = total[...] * shrink + jnp.sum(exp_scores, axis=1, keepdims=True)
            accum[...] = accum[...] * shrink + dot(exp_scores.astype(BF), keys[:, 0:KVL])

    def proj_piece(zz):
        piece = WO.at[pl.ds(pl.multiple_of((yl * 8 + zz) * 32, 32), 32), :]
        return remote(out_proj.at[:, pl.ds(0, SL)], piece, op_s.at[0], op_r.at[zz], (c, e))

    def proj_share(y, zz):
        row = WO.at[pl.ds(pl.multiple_of((y * 8 + zz) * 32, 32), 32), :]
        return remote(row, row, oy_s.at[zz], oy_r.at[zz], (c_y, e))

    own_proj.wait()
    proj_share(yl, z).start()

    def attention_step(m, carry):
        @pl.when(m < 5)
        def _():
            kv_arrive(along(-m), "up", m < 4)

        @pl.when(m < 4)
        def _():
            kv_arrive(along(m), "down", m < 3)

        @pl.when(m < 5)
        def _():
            proj_piece(along(-m)).wait_recv()
            proj_share(yl, along(-m)).start()

        @pl.when(m < 4)
        def _():
            proj_piece(along(m)).wait_recv()
            proj_share(yl, along(m)).start()

        def side(j, carry):
            @pl.when((j == 0) | ((m > 1) & (m < 5)))
            def _():
                attend(along((2 * j - 1) * (m - 1)), m > 1)

            return carry

        lax.fori_loop(0, 2, side, 0)
        return carry

    lax.fori_loop(1, 6, attention_step, 0)

    own_rows = pl.ds(pl.multiple_of(z * 128, 128), 128)
    for h in range(HEAD_DEV):
        rows, columns = slice(h * 128, (h + 1) * 128), slice(h * 128, (h + 1) * 128)
        latent = (accum[rows, :] / total[rows, :]).astype(BF)
        HO[own_rows, columns] = dot(latent, value_up[:, columns]).astype(BF)

    def ho_copy(zz, half, up):
        block = HO.at[pl.ds(pl.multiple_of(zz * 128 + half * 64, 64), 64), :]
        target = yl * 8 + lax.rem(z + (1 if up else 7), 8)
        return remote(
            block, block, (hp_s if up else hm_s).at[zz, half], ho_r.at[zz, half], (target, e)
        )

    for half in range(2):
        ho_copy(z, half, True).start()
        ho_copy(z, half, False).start()
    for zz in range(8):
        proj_share(1 - yl, zz).wait_recv()

    def ho_arrive(zz, up, go_on):
        for half in range(2):
            ho_copy(zz, half, up).wait_recv()

            @pl.when(go_on)
            def _():
                ho_copy(zz, half, up).start()

    def sib_copy(zz):
        return remote(
            PB.at[zz, pl.ds(pl.multiple_of((1 - s) * 64, 64), 64), :],
            SB.at[zz],
            sb_s.at[zz],
            sb_r.at[zz],
            (c, sib),
        )

    below = [lax.rem(z + 8 - t, 8) for t in range(5)]
    above = [lax.rem(z + t, 8) for t in range(4)]

    def ho_pair(t):
        return lax.rem(z + t, 8), lax.rem(z + 7 - t, 8)

    def project(t):
        def one(j, carry):
            za, zb = ho_pair(t)
            zz = jnp.where(j == 0, za, zb)
            PB[zz] = dot(HO[pl.ds(pl.multiple_of(zz * 128, 128), 128), :], WO[...]).astype(BF)
            sib_copy(zz).start()
            return carry

        lax.fori_loop(0, 2, one, 0)

    def rows16(index):
        return pl.ds(pl.multiple_of(index * 16, 16), 16)

    def chip_copy(t, d):
        kk = lax.rem(k + d, 8)
        return remote(
            RED.at[t, rows16(kk), :], RK.at[t, k], rk_s.at[t, d], rk_r.at[t, k], (c, 2 * kk + s)
        )

    def reduce_cores(t):
        for i, zz in enumerate(ho_pair(t)):
            sib_copy(zz).wait_recv()
            own = PB[zz, pl.ds(pl.multiple_of(s * 64, 64), 64), :]
            RED[t, i * 64 : (i + 1) * 64, :] = (own.astype(F32) + SB[zz].astype(F32)).astype(BF)
        for d in range(1, 8):
            chip_copy(t, d).start()
        RK[t, k] = RED[t, rows16(k), :]

    quarter = lax.rem(k, 4)

    def turn_copy(t):
        za, zb = ho_pair(t)
        target = jnp.where(k < 4, za, zb)
        return remote(
            TS.at[t], TR.at[rows16(quarter), :], t_s.at[t], t_r.at[quarter],
            (yl * 8 + target, 2 * z + s),
        )

    def reduce_chips(t):
        for d in range(1, 8):
            kk = lax.rem(k + d, 8)
            remote(TS.at[t], RK.at[t, kk], t_s.at[0], rk_r.at[t, kk], (c, e)).wait_recv()
        summed = RK[t, 0].astype(F32)
        for kk in range(1, 8):
            summed = summed + RK[t, kk].astype(F32)
        TS[t] = summed.astype(BF)
        home = turn_self & (t == 0)

        @pl.when(home)
        def _():
            TR[rows16(quarter), :] = TS[t]

        @pl.when(jnp.logical_not(home))
        def _():
            turn_copy(t).start()

    def down_rows_of(d):
        return WD.at[down_rows(2 * lax.rem(k + d, 8) + s), :]

    def weight_share(kk, core):
        expert = 2 * kk + core
        return remote(W.at[expert], W.at[expert], wf_s.at[kk], wf_r.at[kk], (c, sib))

    def share_weight(d):
        kk = lax.rem(k + d, 8)
        for which in range(2):
            piece = W.at[2 * kk + s, :, pl.ds(which * 128, 128)]
            remote(piece, piece, w_s.at[0, which], w_r.at[kk, which], (c, e)).wait_recv()
        weight_share(kk, s).start()

    for which in range(2):
        own_weight(which).wait()
    weight_share(k, s).start()

    def head_step(t, carry):
        @pl.when(t < 4)
        def _():
            za, zb = ho_pair(t)

            @pl.when(t > 0)
            def _():
                ho_arrive(za, False, t < 3)

            ho_arrive(zb, True, t < 3)
            project(t)

        @pl.when((t > 0) & (t < 5))
        def _():
            reduce_cores(t - 1)

        @pl.when(t > 1)
        def _():
            reduce_chips(t - 2)

        share_weight(t + 1)
        return carry

    lax.fori_loop(0, 6, head_step, 0)

    for j in range(8):

        @pl.when(8 * s + j != e)
        def _():
            remote(HS.at[0], HR.at[j], hd_s.at[0], hd_r.at[j], (c, e)).wait_recv()

    fetch_router.wait()
    for q in range(4):

        @pl.when(jnp.logical_not((z == k) & (turn_base + q == k)))
        def _():
            remote(TS.at[0], TR.at[rows16(q), :], t_s.at[0], t_r.at[q], (c, e)).wait_recv()

    rows_in = HR[...].reshape(TOKENS, 1024)
    residual = (rows_in[:, 0:SL] + TR[...].astype(F32)).astype(BF).astype(F32)
    gains = gain[k]
    lane = iota((TOKENS, META), 1)
    scaled = (residual * gains).astype(BF)
    logits = dot_t(scaled, RT[...])
    squares = jnp.sum(residual * residual, axis=1, keepdims=True)
    ST[k] = jnp.where(lane == EXPERTS, squares, logits)

    def stat_copy(d):
        kk = lax.rem(k + d, 8)
        return remote(ST.at[k], ST.at[k], st_s.at[d], st_r.at[k], (c, 2 * kk + s))

    for d in range(1, 8):
        stat_copy(d).start()
    routed = rows_in[:, SL:1024]
    route0, route1 = column_of(routed, 0), column_of(routed, 1)

    def rows_of(cc):
        return pl.ds(pl.multiple_of(cc * TOKENS, TOKENS), TOKENS)

    X[rows_of(c), 0:SL] = scaled
    X[rows_of(c), SL:1024] = routed.astype(BF)

    def row_copy(cc, way):
        block = X.at[rows_of(cc), :]
        target = {"y": c_y, "up": c_up, "down": c_down}[way]
        sems = {"y": xy_s, "up": xp_s, "down": xm_s}[way]
        return remote(block, block, sems.at[cc], x_r.at[cc], (target, e))

    row_copy(c, "up").start()
    row_copy(c, "down").start()
    row_copy(c, "y").start()

    for d in range(1, 8):
        kk = lax.rem(k + d, 8)
        remote(ST.at[kk], ST.at[kk], st_s.at[0], st_r.at[kk], (c, e)).wait_recv()
    stats = ST[0]
    for kk in range(1, 8):
        stats = stats + ST[kk]
    inverse = lax.rsqrt(column_of(stats, EXPERTS) / D + NORM_EPS)
    affinity = 1.0 / (1.0 + jnp.exp(-(stats * inverse)))
    lane_f = lane.astype(F32)
    chosen0 = jnp.sum(jnp.where(lane_f == route0, affinity, 0.0), axis=1, keepdims=True)
    chosen1 = jnp.sum(jnp.where(lane_f == route1, affinity, 0.0), axis=1, keepdims=True)
    scale = ROUTE_SCALE / (chosen0 + chosen1)
    MS[...] = jnp.where(
        lane == 0, chosen0 * scale, jnp.where(lane == 1, chosen1 * scale, inverse)
    )
    scale_half = lax.rem(k, 2)

    def scale_copy(y, t):
        target = jnp.where(k < 4, along(-t), along(1 + t))
        return remote(
            MS.at[pl.ds(pl.multiple_of(scale_half * 32, 32), 32), :], MR.at[t], ms_s.at[y, t],
            ms_r.at[t], (y * 8 + target, e),
        )

    def scale_stays(y, t):
        return (k < 4) & (t == 0) & (y == yl)

    @pl.when(yl == scale_row)
    def _():
        for t in range(4):
            for y in range(2):

                @pl.when(jnp.logical_not(scale_stays(y, t)))
                def _():
                    scale_copy(y, t).start()

                @pl.when(scale_stays(y, t))
                def _():
                    MR[t] = MS[pl.ds(pl.multiple_of(scale_half * 32, 32), 32), :]

    row_copy(c_y, "y").wait_recv()

    row_copy(c_y, "up").start()
    row_copy(c_y, "down").start()

    def arrive(zz, way, go_on):
        own, other = yl * 8 + zz, (1 - yl) * 8 + zz
        row_copy(own, way).wait_recv()

        @pl.when(go_on)
        def _():
            row_copy(own, way).start()

        row_copy(other, way).wait_recv()

        @pl.when(go_on)
        def _():
            row_copy(other, way).start()

    def chunk(t):
        return along(t), along(-1 - t)

    def places(t):
        za, zb = chunk(t)
        return [(0, za), (1, za), (0, zb), (1, zb)]

    def part(kk):
        return pl.ds(pl.multiple_of(kk * 32, 32), 32)

    def half_copy(t, d):
        kk = lax.rem(k + d, 8)
        return remote(
            GS.at[t, :, part(kk), :], GR.at[t, k], g_s.at[t, d], g_r.at[t, k], (c, 2 * kk + s)
        )

    def first_layers(t):
        for i, (y, zz) in enumerate(places(t)):
            XC[t, i * 64 : (i + 1) * 64, :] = X[rows_of(y * 8 + zz), :]
        acc0[...] = jnp.zeros(acc0.shape, F32)
        acc1[...] = jnp.zeros(acc1.shape, F32)
        routed_here = XC[t, :, SL:1024].astype(F32)
        r0, r1 = column_of(routed_here, 0), column_of(routed_here, 1)

        def one_expert(expert, carry):
            product = dot(XC[t, :, 0:SL], W[expert])
            number = expert.astype(F32)
            acc0[...] += jnp.where(r0 == number, product, 0.0)
            acc1[...] += jnp.where(r1 == number, product, 0.0)
            return carry

        lax.fori_loop(0, EXPERTS, one_expert, 0)
        GS[t, 0] = acc0[...].astype(BF)
        GS[t, 1] = acc1[...].astype(BF)
        for d in range(1, 8):
            half_copy(t, d).start()
        GR[t, k] = GS[t, :, part(k), :]

    def act_copy(t, d):
        kk = lax.rem(k + d, 8)
        block = A.at[t, :, part(k), :]
        return remote(block, block, a_s.at[t, d], a_r.at[t, k], (c, 2 * kk + s))

    def activate(t):
        for d in range(1, 8):
            kk = lax.rem(k + d, 8)
            remote(GR.at[t, k], GR.at[t, kk], g_s.at[t, 0], g_r.at[t, kk], (c, e)).wait_recv()
        @pl.when(scale_source(t) != c)
        def _():
            remote(MR.at[t], MR.at[t], ms_s.at[0, 0], ms_r.at[t], (c, e)).wait_recv()

        here = MR[t]
        inverse_here = column_of(here, 2)
        for r in range(2):
            both = GR[t, 0, r].astype(F32)
            for kk in range(1, 8):
                both = both + GR[t, kk, r].astype(F32)
            both = both * inverse_here
            weight = column_of(here, r)
            gate, up = both[:, 0:128], both[:, 128:256]
            A[t, r, part(k), :] = (gate / (1.0 + jnp.exp(-gate)) * up * weight).astype(BF)
        for d in range(1, 8):
            act_copy(t, d).start()

    def partner_copy(y, zz):
        return remote(DP.at[zz, y], YB.at[zz], yb_s.at[zz], yb_r.at[zz], (c_y, e))

    def second_layer(t):
        for d in range(1, 8):
            kk = lax.rem(k + d, 8)
            block = A.at[t, :, part(kk), :]
            remote(block, block, a_s.at[t, 0], a_r.at[t, kk], (c, e)).wait_recv()
        routed_here = XC[t, :, SL:1024].astype(F32)
        r0, r1 = column_of(routed_here, 0), column_of(routed_here, 1)
        a0, a1 = A[t, 0].astype(F32), A[t, 1].astype(F32)
        for expert in range(EXPERTS):
            picked = jnp.where(r0 == float(expert), a0, 0.0) + jnp.where(
                r1 == float(expert), a1, 0.0
            )
            AC[:, expert * 128 : (expert + 1) * 128] = picked.astype(BF)
        out = dot(AC[...], WD[...])
        for i, (y, zz) in enumerate(places(t)):
            DP[zz, y] = out[i * 64 : (i + 1) * 64, :].astype(BF)

        @pl.when(s == 1)
        def _():
            for zz in chunk(t):
                partner_copy(1 - yl, zz).start()

    def down_share(kk, core):
        block = WD.at[down_rows(2 * kk + core), :]
        return remote(block, block, df_s.at[kk], df_r.at[kk], (c, sib))

    arrive(near[1], "up", True)
    share_weight(7)

    def layer_step(t, carry):
        @pl.when(t < 3)
        def _():
            arrive(along(t + 1), "down", t < 2)
            arrive(along(-2 - t), "up", t < 2)

        @pl.when(t == 0)
        def _():
            for kk in range(8):
                weight_share(kk, 1 - s).wait_recv()
            for d in range(1, 8):
                down_weight(d).start()

        @pl.when(t < 4)
        def _():
            first_layers(t)

        @pl.when(t == 1)
        def _():
            own_down.wait()
            down_share(k, s).start()
            for d in range(1, 8):
                block = down_rows_of(d)
                kk = lax.rem(k + d, 8)
                remote(block, block, d_s.at[0], d_r.at[kk], (c, e)).wait_recv()
                down_share(kk, s).start()

        @pl.when((t > 0) & (t < 5))
        def _():
            activate(t - 1)

        @pl.when(t == 2)
        def _():
            for kk in range(8):
                down_share(kk, 1 - s).wait_recv()

        @pl.when(t > 1)
        def _():
            second_layer(t - 2)

        return carry

    lax.fori_loop(0, 6, layer_step, 0)

    routed_all = X[:, SL:1024].astype(F32)
    lane_all = iota(routed_all.shape, 1).astype(F32)
    named = jnp.where(lane_all == column_of(routed_all, 0), 1.0, 0.0) + jnp.where(
        lane_all == column_of(routed_all, 1), 1.0, 0.0
    )
    CS[...] = jnp.broadcast_to(jnp.sum(named, axis=0, keepdims=True), CS.shape)
    count_copy = remote(CS, CR, c_s.at[0], c_r.at[0], (c, sib))
    count_copy.start()

    def joins(y):
        return (s == 0) | (y == yl)

    def complete(zz):
        @pl.when(s == 1)
        def _():
            partner_copy(yl, zz).wait_recv()
            DP[zz, yl] = (DP[zz, yl].astype(F32) + YB[zz].astype(F32)).astype(BF)

    def up_copy(source, step, y):
        return remote(source, RP.at[step, y], p_s.at[step, y], p_r.at[step, y], (c_up, e))

    def down_copy(source, step, y):
        return remote(source, RM.at[step, y], m_s.at[step, y], m_r.at[step, y], (c_down, e))

    ups = [along(4 - t) for t in range(5)]
    downs = [along(t - 3) for t in range(4)]
    complete(ups[0])
    complete(downs[0])
    for y in range(2):

        @pl.when(joins(y))
        def _():
            up_copy(DP.at[ups[0], y], 0, y).start()
            down_copy(DP.at[downs[0], y], 0, y).start()

    for t in range(1, 4):
        complete(ups[t])
        complete(downs[t])
        for y in range(2):

            @pl.when(joins(y))
            def _():
                up_copy(SP.at[0, y], t - 1, y).wait_recv()
                SP[t - 1, y] = (
                    DP[ups[t], y].astype(F32) + RP[t - 1, y].astype(F32)
                ).astype(BF)
                up_copy(SP.at[t - 1, y], t, y).start()
                if t < 3:
                    down_copy(SM.at[0, y], t - 1, y).wait_recv()
                    SM[t - 1, y] = (
                        DP[downs[t], y].astype(F32) + RM[t - 1, y].astype(F32)
                    ).astype(BF)
                    down_copy(SM.at[t - 1, y], t, y).start()

    def final(y):
        down_copy(SM.at[0, 0], 2, y).wait_recv()
        up_copy(SP.at[0, 0], 3, y).wait_recv()
        return DP[z, y].astype(F32) + RP[3, y].astype(F32) + RM[2, y].astype(F32)

    y_copy = remote(YS, YR, y_s.at[0], y_r.at[0], (c_y, e))

    @pl.when(s == 0)
    def _():
        YS[...] = final(1 - yl).astype(BF)
        y_copy.start()

    OS[...] = final(yl) + residual

    @pl.when(s == 0)
    def _():
        y_copy.wait_recv()
        OS[...] += YR[...].astype(F32)

    def owner_copy(j):
        return remote(
            OS.at[pl.ds(j * 8, 8), :], OR.at[k], o_s.at[j], o_r.at[k], (c, 8 * s + j)
        )

    for j in range(8):

        @pl.when(8 * s + j != e)
        def _():
            owner_copy(j).start()

        @pl.when(8 * s + j == e)
        def _():
            OR[k] = OS[pl.ds(j * 8, 8), :]

    count_copy.wait_recv()
    counts = (CS[...] + CR[...])[0:1, 0:EXPERTS]
    load_out[...] = LOAD_DECAY * ema[...] + (1.0 - LOAD_DECAY) * counts / 256.0

    for zz in range(8):
        sib_copy(zz).wait_send()
        weight_share(zz, s).wait_send()
        down_share(zz, s).wait_send()

        @pl.when(2 * zz + e_half != e)
        def _():
            hidden_copy(zz).wait_send()

        @pl.when(s == 1)
        def _():
            partner_copy(1 - yl, zz).wait_send()

    for d in range(1, 8):
        proj_copy(d).wait_send()
        down_weight(d).wait_send()
        stat_copy(d).wait_send()
        for which in range(2):
            weight_copy(d, which).wait_send()
        for t in range(4):
            chip_copy(t, d).wait_send()
            half_copy(t, d).wait_send()
            act_copy(t, d).wait_send()
    for zz in range(8):
        proj_share(yl, zz).wait_send()

    @pl.when(jnp.logical_not(turn_self))
    def _():
        turn_copy(0).wait_send()

    for t in range(1, 4):
        turn_copy(t).wait_send()
    for half in range(2):
        for t in range(4):
            ho_copy(below[t], half, True).wait_send()
        for t in range(3):
            ho_copy(above[t], half, False).wait_send()

    both_rows = yl == 1
    for t in range(8):
        zz = lax.rem(z + t, 8)
        if t > 0:
            kv_share(yl, zz, s).wait_send()

        @pl.when(yl == 1)
        def _():
            kv_share(0, zz, s).wait_send()

        @pl.when((yl == 0) & (zz == z))
        def _():
            kv_copy(0, zz, "y").wait_send()

        @pl.when(zz == z)
        def _():
            row_copy(yl * 8 + zz, "y").wait_send()

    for t in range(4):
        kv_copy(yl, near[t], "up").wait_send()
        row_copy(yl * 8 + near[t], "up").wait_send()

        @pl.when(both_rows)
        def _():
            kv_copy(0, near[t], "up").wait_send()

        row_copy((1 - yl) * 8 + near[t], "up").wait_send()

    for t in range(3):
        kv_copy(yl, far[t], "down").wait_send()
        row_copy(yl * 8 + far[t], "down").wait_send()

        @pl.when(both_rows)
        def _():
            kv_copy(0, far[t], "down").wait_send()

        row_copy((1 - yl) * 8 + far[t], "down").wait_send()

    for y in range(2):

        @pl.when(joins(y))
        def _():
            up_copy(DP.at[ups[0], y], 0, y).wait_send()
            down_copy(DP.at[downs[0], y], 0, y).wait_send()
            for t in range(1, 4):
                up_copy(SP.at[t - 1, y], t, y).wait_send()
                if t < 3:
                    down_copy(SM.at[t - 1, y], t, y).wait_send()

    @pl.when(s == 0)
    def _():
        y_copy.wait_send()

    count_copy.wait_send()

    @pl.when(yl == scale_row)
    def _():
        for t in range(4):
            for y in range(2):

                @pl.when(jnp.logical_not(scale_stays(y, t)))
                def _():
                    scale_copy(y, t).wait_send()

    for j in range(8):

        @pl.when(8 * s + j != e)
        def _():
            owner_copy(j).wait_send()

    for kk in range(8):

        @pl.when(2 * kk + e_half != e)
        def _():
            remote(
                OS.at[pl.ds(0, 8), :], OR.at[kk], o_s.at[0], o_r.at[kk], (c, e)
            ).wait_recv()

        layer_out[:, kk * SL : (kk + 1) * SL] = OR[kk].astype(BF)


def in_vmem(count):
    return [pl.BlockSpec(memory_space=pltpu.VMEM)] * count


def anywhere(count):
    return [pl.BlockSpec(memory_space=pl.ANY)] * count


def dma(*shape):
    return pltpu.SemaphoreType.DMA(shape)


def shaped(shape, dtype):
    return jax.ShapeDtypeStruct(shape, dtype)


def params(number):
    return pltpu.CompilerParams(
        collective_id=number, has_side_effects=True, vmem_limit_bytes=VMEM_LIMIT
    )


def body(
    hidden, q_nope, q_rope, kv_latent, k_rope, key_up, value_up, out_proj, ffn_gain, router,
    w_gate, w_up, w_down, routes, load_ema,
):
    v = pltpu.VMEM
    layer_out, new_load = pl.pallas_call(
        layer_kernel,
        out_shape=(shaped((8, D), BF), shaped((1, EXPERTS), F32)),
        in_specs=in_vmem(10) + anywhere(5),
        out_specs=tuple(in_vmem(2)),
        scratch_shapes=[
            v((2048, 640), BF), v((512, 640), BF), v((512, 1), F32), v((512, 1), F32),
            v((512, 512), F32), v((1024, 512), BF), v((512, SL), BF), v((8, 128, SL), BF),
            v((8, 64, SL), BF), v((4, 128, SL), BF), v((4, 8, 16, SL), BF), v((4, 16, SL), BF),
            v((64, SL), BF), v((8, 8, 1024), F32), v((8, 8, 1024), F32),
            v((1024, 1024), BF), v((16, SL, 256), BF), v((128, SL), BF), v((8, 64, META), F32),
            v((4, 256, 1024), BF), v((256, 256), F32), v((256, 256), F32),
            v((4, 2, 256, 256), BF), v((4, 8, 2, 32, 256), BF), v((4, 2, 256, 128), BF),
            v((2048, SL), BF), v((256, 2048), BF), v((8, 2, 64, SL), BF), v((8, 64, SL), BF),
            v((4, 2, 64, SL), BF), v((3, 2, 64, SL), BF), v((3, 2, 64, SL), BF),
            v((2, 2, 64, SL), BF), v((64, SL), BF), v((64, SL), BF), v((64, SL), F32),
            v((8, 8, SL), F32), v((8, 128), F32), v((8, 128), F32), v((64, META), F32),
            v((4, 32, META), F32),
            dma(5), dma(16), dma(16), dma(16), dma(16), dma(16), dma(16), dma(8), dma(8),
            dma(8), dma(8), dma(8), dma(8),
            dma(8, 2), dma(8, 2), dma(8), dma(8), dma(8, 2), dma(8, 2), dma(8, 2), dma(8), dma(8),
            dma(4, 8), dma(4, 8), dma(4), dma(4),
            dma(8), dma(8), dma(8), dma(8), dma(8), dma(8), dma(16), dma(16), dma(16), dma(16),
            dma(4, 8), dma(4, 8), dma(4, 8), dma(4, 8),
            dma(8), dma(8), dma(4, 2), dma(4, 2), dma(3, 2), dma(3, 2), dma(1), dma(1), dma(8),
            dma(8), dma(1), dma(1), dma(2, 4), dma(4),
        ],
        compiler_params=params(0),
        name="layer",
    )(
        q_nope, q_rope, kv_latent, k_rope.T, key_up, value_up, hidden, routes.T,
        ffn_gain.reshape(8, 1, SL), load_ema.reshape(1, EXPERTS), out_proj, router.T, w_gate, w_up, w_down,
    )
    return layer_out, new_load.reshape(EXPERTS)


def solution(mesh):
    placed = (
        P(("ctx", "ep"), None),
        P("ctx", "ep"),
        P("ctx", "ep"),
        P("ctx", None),
        P("ctx", None),
        P(None, "ep"),
        P(None, "ep"),
        P(("ep", "ctx"), None),
        P(),
        P(),
        P("ep", None, "ctx"),
        P("ep", None, "ctx"),
        P("ep", "ctx", None),
        P(("ctx", "ep"), None),
        P(),
    )
    return jax.shard_map(
        body, mesh=mesh, in_specs=placed, out_specs=(P(("ctx", "ep"), None), P()), check_vma=False
    )
```

```python
import functools

import jax
import jax.numpy as jnp
from jax import lax
from jax.experimental import pallas as pl
from jax.experimental.pallas import tpu as pltpu
from jax.sharding import PartitionSpec as P

D = 7168
KVL = 512
NOPE = 128
ROPE = 64
VDIM = 128
HEAD_DEV = 4
SL = 896
EXPERTS = 16
META = 128
TOKENS = 64

SCORE_FLOOR = -1e30
NORM_EPS = 1e-06
ROUTE_SCALE = 2.5
LOAD_DECAY = 0.5
MESH = pl.DeviceIdType.MESH
BF = jnp.bfloat16
F32 = jnp.float32
VMEM_LIMIT = 56 * 2**20


def place():
    c = lax.axis_index("ctx")
    e = lax.axis_index("ep")
    return c, e, lax.div(c, 8), lax.rem(c, 8), lax.div(e, 2), lax.rem(e, 2)


def remote(src, dst, send, recv, device):
    return pltpu.make_async_remote_copy(
        src_ref=src, dst_ref=dst, send_sem=send, recv_sem=recv, device_id=device, device_id_type=MESH
    )


def dot(a, b):
    return jnp.dot(a, b, preferred_element_type=F32)


def dot_t(a, b):
    return lax.dot_general(a, b, (((1,), (1,)), ((), ())), preferred_element_type=F32)


def iota(shape, dim):
    return lax.broadcasted_iota(jnp.int32, shape, dim)


def selector(rows, columns, shift, width):
    row, column = iota((rows, columns), 0), iota((rows, columns), 1)
    return jnp.where((row == column + shift) & (column < width), 1.0, 0.0).astype(BF)


def column_of(block, index):
    return jnp.sum(jnp.where(iota(block.shape, 1) == index, block, 0.0), axis=1, keepdims=True)


def layer_kernel(
    q_nope, q_rope, kv, k_rope, key_up, value_up, hidden, routes, gain, ema, out_proj, router, w_gate, w_up, w_down,
    layer_out, load_out,
    KV, Q, top, total, accum, HO, WO, PB, SB, RED, RK, TS, TR, HS, HR,
    X, W, RT, ST, XC, acc0, acc1, GS, GR, A, WD, AC, DP, YB, RP, RM, SP, SM, YS, YR, OS, OR, CS, CR, MS, MR,
    local, kp_s, km_s, ky_s, kv_r, kf_s, kf_r, op_s, op_r, oy_s, oy_r, hd_s, hd_r,
    w_s, w_r, wf_s, wf_r, hp_s, hm_s, ho_r, sb_s, sb_r, rk_s, rk_r, t_s, t_r,
    st_s, st_r, d_s, d_r, df_s, df_r, xp_s, xm_s, xy_s, x_r, g_s, g_r, a_s, a_r,
    yb_s, yb_r, p_s, p_r, m_s, m_r, y_s, y_r, o_s, o_r, c_s, c_r, ms_s, ms_r,
):
    c, e, yl, z, k, s = place()
    sib = 2 * k + 1 - s
    e_half, e_row = lax.div(e, 8), lax.rem(e, 8)
    c_y = (1 - yl) * 8 + z
    sign = 1 - 2 * s

    def along(t):
        return lax.rem(z + 8 + sign * t, 8)

    c_up, c_down = yl * 8 + along(1), yl * 8 + along(-1)
    near = [along(-t) for t in range(5)]
    far = [along(t) for t in range(4)]

    def kv_rows(slot, start, size):
        return pl.ds(pl.multiple_of(slot * 128 + start, 64), size)

    def kv_slot(y, zz):
        return 2 * zz + y

    own_slot = kv_slot(yl, z)
    KV[kv_rows(own_slot, 0, 128), 0:KVL] = kv[...]
    KV[kv_rows(own_slot, 0, 128), KVL:640] = lax.dot_general(
        k_rope[...], selector(ROPE, 128, 0, ROPE), (((0,), (0,)), ((), ())),
        preferred_element_type=F32,
    ).astype(BF)

    @pl.when(yl == 0)
    def _():
        for zz in range(8):
            KV[kv_rows(kv_slot(1, zz), 0, 128), :] = jnp.zeros((128, 640), BF)

    diagonal = iota((8, 8), 0) == iota((8, 8), 1)
    route_columns = [
        jnp.sum(jnp.where(diagonal, routes[r : r + 1, :], 0), axis=1, keepdims=True)
        for r in range(2)
    ]
    route_block = jnp.where(
        iota((8, META), 1) == 0,
        route_columns[0],
        jnp.where(iota((8, META), 1) == 1, route_columns[1], 0),
    ).astype(F32)
    for kk in range(8):
        HS[kk, :, 0:SL] = hidden[:, kk * SL : (kk + 1) * SL].astype(F32)
        HS[kk, :, SL:1024] = route_block

    barrier = pltpu.get_barrier_semaphore()

    def greet(device):
        pl.semaphore_signal(barrier, 1, device_id=device, device_id_type=MESH)

    for d in range(1, 8):
        greet((yl * 8 + lax.rem(z + d, 8), e))
    greet((c_y, e))
    for d in range(1, 16):
        greet((c, lax.rem(e + d, 16)))
    turn_base = jnp.where(lax.rem(z + 8 - k, 8) < 4, 0, 4)
    turn_self = (z == k) & (k < 4)
    for q in range(4):

        @pl.when(jnp.logical_not((z == k) & (turn_base + q == k)))
        def _():
            greet((yl * 8 + k, 2 * (turn_base + q) + s))

    scale_row = lax.rem(lax.div(k, 2), 2)

    def scale_source(t):
        return scale_row * 8 + jnp.where(k < 4, along(t), along(-1 - t))

    for t in range(4):

        @pl.when(scale_source(t) != c)
        def _():
            greet((scale_source(t), e))

    scale_sends = jnp.where(yl == scale_row, jnp.where(k < 4, 7, 8), 0)
    pl.semaphore_wait(barrier, 27 - turn_self.astype(jnp.int32) + scale_sends)

    def kv_copy(y, zz, way):
        block = KV.at[kv_rows(kv_slot(y, zz), s * 64, 64), :]
        target = {"y": c_y, "up": c_up, "down": c_down}[way]
        sems = {"y": ky_s, "up": kp_s, "down": km_s}[way]
        slot = kv_slot(y, zz)
        return remote(block, block, sems.at[slot], kv_r.at[slot], (target, e))

    def kv_share(y, zz, core):
        slot = kv_slot(y, zz)
        block = KV.at[kv_rows(slot, core * 64, 64), :]
        return remote(block, block, kf_s.at[slot], kf_r.at[slot], (c, sib))

    kv_copy(yl, z, "up").start()
    kv_copy(yl, z, "down").start()

    @pl.when(yl == 0)
    def _():
        kv_copy(0, z, "y").start()

    def proj_copy(d):
        zz = lax.rem(z + d, 8)
        return remote(
            out_proj.at[:, pl.ds(pl.multiple_of(zz * SL, 128), SL)],
            WO.at[pl.ds(pl.multiple_of(c * 32, 32), 32), :],
            op_s.at[d],
            op_r.at[z],
            (yl * 8 + zz, e),
        )

    own_proj = pltpu.make_async_copy(
        out_proj.at[:, pl.ds(pl.multiple_of(z * SL, 128), SL)],
        WO.at[pl.ds(pl.multiple_of(c * 32, 32), 32), :],
        local.at[0],
    )
    own_proj.start()
    for d in range(1, 8):
        proj_copy(d).start()

    def hidden_copy(kk):
        return remote(
            HS.at[kk], HR.at[e_row], hd_s.at[kk], hd_r.at[e_row], (c, 2 * kk + e_half)
        )

    for kk in range(8):

        @pl.when(2 * kk + e_half != e)
        def _():
            hidden_copy(kk).start()

        @pl.when(2 * kk + e_half == e)
        def _():
            HR[e_row] = HS[kk]

    def weight_copy(d, which):
        kk = lax.rem(k + d, 8)
        source = (w_gate, w_up)[which]
        return remote(
            source.at[0, pl.ds(pl.multiple_of(kk * SL, SL), SL), :],
            W.at[e, :, pl.ds(which * 128, 128)],
            w_s.at[d, which],
            w_r.at[k, which],
            (c, 2 * kk + s),
        )

    def own_weight(which):
        source = (w_gate, w_up)[which]
        return pltpu.make_async_copy(
            source.at[0, pl.ds(pl.multiple_of(k * SL, SL), SL), :],
            W.at[e, :, pl.ds(which * 128, 128)],
            local.at[1 + which],
        )

    for which in range(2):
        own_weight(which).start()
    for d in (4, 3, 5, 2, 6, 1, 7):
        for which in range(2):
            weight_copy(d, which).start()
    RT[...] = jnp.zeros(RT.shape, BF)
    fetch_router = pltpu.make_async_copy(
        router.at[:, pl.ds(pl.multiple_of(k * SL, 128), SL)], RT.at[pl.ds(0, EXPERTS), :], local.at[3]
    )
    fetch_router.start()

    def down_rows(expert):
        return pl.ds(pl.multiple_of(expert * 128, 128), 128)

    def down_weight(d):
        kk = lax.rem(k + d, 8)
        return remote(
            w_down.at[0, :, pl.ds(pl.multiple_of(kk * SL, 128), SL)],
            WD.at[down_rows(e), :],
            d_s.at[d],
            d_r.at[k],
            (c, 2 * kk + s),
        )

    own_down = pltpu.make_async_copy(
        w_down.at[0, :, pl.ds(pl.multiple_of(k * SL, 128), SL)], WD.at[down_rows(e), :], local.at[4]
    )
    own_down.start()

    for h in range(HEAD_DEV):
        rows, columns = slice(h * 128, (h + 1) * 128), slice(h * 128, (h + 1) * 128)
        Q[rows, 0:KVL] = dot_t(q_nope[:, columns], key_up[:, columns]).astype(BF)
        Q[rows, KVL:640] = dot(
            q_rope[...], selector(HEAD_DEV * ROPE, 128, h * ROPE, ROPE)
        ).astype(BF)
    top[...] = jnp.full(top.shape, SCORE_FLOOR, F32)
    total[...] = jnp.zeros(total.shape, F32)
    accum[...] = jnp.zeros(accum.shape, F32)

    @pl.when(yl == 1)
    def _():
        kv_copy(0, z, "y").wait_recv()
        kv_share(0, z, s).start()

        kv_copy(0, z, "up").start()
        kv_copy(0, z, "down").start()

    def kv_arrive(zz, way, go_on):
        kv_copy(yl, zz, way).wait_recv()

        @pl.when(go_on)
        def _():
            kv_copy(yl, zz, way).start()

        kv_share(yl, zz, s).start()

        @pl.when(yl == 1)
        def _():
            kv_copy(0, zz, way).wait_recv()
            kv_share(0, zz, s).start()

            @pl.when(go_on)
            def _():
                kv_copy(0, zz, way).start()

    score_scale = (NOPE + ROPE) ** (-0.5)

    def attend(zz, shared):
        @pl.when(shared)
        def _():
            kv_share(yl, zz, 1 - s).wait_recv()

        @pl.when(yl == 1)
        def _():
            kv_share(0, zz, 1 - s).wait_recv()

        @pl.when((yl == 1) | (zz <= z))
        def _():
            keys = KV[pl.ds(pl.multiple_of(zz * 256, 256), 256), :]
            scores = dot_t(Q[...], keys)
            query_pos = c * 128 + (iota(scores.shape, 0) & 127)
            column = iota(scores.shape, 1)
            key_pos = zz * 128 + jnp.where(column < 128, column, column + (1024 - 128))
            scores = jnp.where(key_pos <= query_pos, scores, SCORE_FLOOR)
            top_old = top[...]
            top_new = jnp.maximum(top_old, jnp.max(scores, axis=1, keepdims=True))
            exp_scores = jnp.exp((scores - top_new) * score_scale)
            shrink = jnp.exp((top_old - top_new) * score_scale)
            top[...] = top_new
            total[...] = total[...] * shrink + jnp.sum(exp_scores, axis=1, keepdims=True)
            accum[...] = accum[...] * shrink + dot(exp_scores.astype(BF), keys[:, 0:KVL])

    def proj_piece(zz):
        piece = WO.at[pl.ds(pl.multiple_of((yl * 8 + zz) * 32, 32), 32), :]
        return remote(out_proj.at[:, pl.ds(0, SL)], piece, op_s.at[0], op_r.at[zz], (c, e))

    def proj_share(y, zz):
        row = WO.at[pl.ds(pl.multiple_of((y * 8 + zz) * 32, 32), 32), :]
        return remote(row, row, oy_s.at[zz], oy_r.at[zz], (c_y, e))

    own_proj.wait()
    proj_share(yl, z).start()

    def attention_step(m, carry):
        @pl.when(m < 5)
        def _():
            kv_arrive(along(-m), "up", m < 4)

        @pl.when(m < 4)
        def _():
            kv_arrive(along(m), "down", m < 3)

        @pl.when(m < 5)
        def _():
            proj_piece(along(-m)).wait_recv()
            proj_share(yl, along(-m)).start()

        @pl.when(m < 4)
        def _():
            proj_piece(along(m)).wait_recv()
            proj_share(yl, along(m)).start()

        def side(j, carry):
            @pl.when((j == 0) | ((m > 1) & (m < 5)))
            def _():
                attend(along((2 * j - 1) * (m - 1)), m > 1)

            return carry

        lax.fori_loop(0, 2, side, 0)
        return carry

    lax.fori_loop(1, 6, attention_step, 0)

    own_rows = pl.ds(pl.multiple_of(z * 128, 128), 128)
    for h in range(HEAD_DEV):
        rows, columns = slice(h * 128, (h + 1) * 128), slice(h * 128, (h + 1) * 128)
        latent = (accum[rows, :] / total[rows, :]).astype(BF)
        HO[own_rows, columns] = dot(latent, value_up[:, columns]).astype(BF)

    def ho_copy(zz, half, up):
        block = HO.at[pl.ds(pl.multiple_of(zz * 128 + half * 64, 64), 64), :]
        target = yl * 8 + lax.rem(z + (1 if up else 7), 8)
        return remote(
            block, block, (hp_s if up else hm_s).at[zz, half], ho_r.at[zz, half], (target, e)
        )

    for half in range(2):
        ho_copy(z, half, True).start()
        ho_copy(z, half, False).start()
    for zz in range(8):
        proj_share(1 - yl, zz).wait_recv()

    def ho_arrive(zz, up, go_on):
        for half in range(2):
            ho_copy(zz, half, up).wait_recv()

            @pl.when(go_on)
            def _():
                ho_copy(zz, half, up).start()

    def sib_copy(zz):
        return remote(
            PB.at[zz, pl.ds(pl.multiple_of((1 - s) * 64, 64), 64), :],
            SB.at[zz],
            sb_s.at[zz],
            sb_r.at[zz],
            (c, sib),
        )

    below = [lax.rem(z + 8 - t, 8) for t in range(5)]
    above = [lax.rem(z + t, 8) for t in range(4)]

    def ho_pair(t):
        return lax.rem(z + t, 8), lax.rem(z + 7 - t, 8)

    def project(t):
        def one(j, carry):
            za, zb = ho_pair(t)
            zz = jnp.where(j == 0, za, zb)
            PB[zz] = dot(HO[pl.ds(pl.multiple_of(zz * 128, 128), 128), :], WO[...]).astype(BF)
            sib_copy(zz).start()
            return carry

        lax.fori_loop(0, 2, one, 0)

    def rows16(index):
        return pl.ds(pl.multiple_of(index * 16, 16), 16)

    def chip_copy(t, d):
        kk = lax.rem(k + d, 8)
        return remote(
            RED.at[t, rows16(kk), :], RK.at[t, k], rk_s.at[t, d], rk_r.at[t, k], (c, 2 * kk + s)
        )

    def reduce_cores(t):
        for i, zz in enumerate(ho_pair(t)):
            sib_copy(zz).wait_recv()
            own = PB[zz, pl.ds(pl.multiple_of(s * 64, 64), 64), :]
            RED[t, i * 64 : (i + 1) * 64, :] = (own.astype(F32) + SB[zz].astype(F32)).astype(BF)
        for d in range(1, 8):
            chip_copy(t, d).start()
        RK[t, k] = RED[t, rows16(k), :]

    quarter = lax.rem(k, 4)

    def turn_copy(t):
        za, zb = ho_pair(t)
        target = jnp.where(k < 4, za, zb)
        return remote(
            TS.at[t], TR.at[rows16(quarter), :], t_s.at[t], t_r.at[quarter],
            (yl * 8 + target, 2 * z + s),
        )

    def reduce_chips(t):
        for d in range(1, 8):
            kk = lax.rem(k + d, 8)
            remote(TS.at[t], RK.at[t, kk], t_s.at[0], rk_r.at[t, kk], (c, e)).wait_recv()
        summed = RK[t, 0].astype(F32)
        for kk in range(1, 8):
            summed = summed + RK[t, kk].astype(F32)
        TS[t] = summed.astype(BF)
        home = turn_self & (t == 0)

        @pl.when(home)
        def _():
            TR[rows16(quarter), :] = TS[t]

        @pl.when(jnp.logical_not(home))
        def _():
            turn_copy(t).start()

    def down_rows_of(d):
        return WD.at[down_rows(2 * lax.rem(k + d, 8) + s), :]

    def weight_share(kk, core):
        expert = 2 * kk + core
        return remote(W.at[expert], W.at[expert], wf_s.at[kk], wf_r.at[kk], (c, sib))

    def share_weight(d):
        kk = lax.rem(k + d, 8)
        for which in range(2):
            piece = W.at[2 * kk + s, :, pl.ds(which * 128, 128)]
            remote(piece, piece, w_s.at[0, which], w_r.at[kk, which], (c, e)).wait_recv()
        weight_share(kk, s).start()

    for which in range(2):
        own_weight(which).wait()
    weight_share(k, s).start()

    def head_step(t, carry):
        @pl.when(t < 4)
        def _():
            za, zb = ho_pair(t)

            @pl.when(t > 0)
            def _():
                ho_arrive(za, False, t < 3)

            ho_arrive(zb, True, t < 3)
            project(t)

        @pl.when((t > 0) & (t < 5))
        def _():
            reduce_cores(t - 1)

        @pl.when(t > 1)
        def _():
            reduce_chips(t - 2)

        share_weight(t + 1)
        return carry

    lax.fori_loop(0, 6, head_step, 0)

    for j in range(8):

        @pl.when(8 * s + j != e)
        def _():
            remote(HS.at[0], HR.at[j], hd_s.at[0], hd_r.at[j], (c, e)).wait_recv()

    fetch_router.wait()
    for q in range(4):

        @pl.when(jnp.logical_not((z == k) & (turn_base + q == k)))
        def _():
            remote(TS.at[0], TR.at[rows16(q), :], t_s.at[0], t_r.at[q], (c, e)).wait_recv()

    rows_in = HR[...].reshape(TOKENS, 1024)
    residual = (rows_in[:, 0:SL] + TR[...].astype(F32)).astype(BF).astype(F32)
    gains = gain[k]
    lane = iota((TOKENS, META), 1)
    scaled = (residual * gains).astype(BF)
    logits = dot_t(scaled, RT[...])
    squares = jnp.sum(residual * residual, axis=1, keepdims=True)
    ST[k] = jnp.where(lane == EXPERTS, squares, logits)

    def stat_copy(d):
        kk = lax.rem(k + d, 8)
        return remote(ST.at[k], ST.at[k], st_s.at[d], st_r.at[k], (c, 2 * kk + s))

    for d in range(1, 8):
        stat_copy(d).start()
    routed = rows_in[:, SL:1024]
    route0, route1 = column_of(routed, 0), column_of(routed, 1)

    def rows_of(cc):
        return pl.ds(pl.multiple_of(cc * TOKENS, TOKENS), TOKENS)

    X[rows_of(c), 0:SL] = scaled
    X[rows_of(c), SL:1024] = routed.astype(BF)

    def row_copy(cc, way):
        block = X.at[rows_of(cc), :]
        target = {"y": c_y, "up": c_up, "down": c_down}[way]
        sems = {"y": xy_s, "up": xp_s, "down": xm_s}[way]
        return remote(block, block, sems.at[cc], x_r.at[cc], (target, e))

    row_copy(c, "up").start()
    row_copy(c, "down").start()
    row_copy(c, "y").start()

    for d in range(1, 8):
        kk = lax.rem(k + d, 8)
        remote(ST.at[kk], ST.at[kk], st_s.at[0], st_r.at[kk], (c, e)).wait_recv()
    stats = ST[0]
    for kk in range(1, 8):
        stats = stats + ST[kk]
    inverse = lax.rsqrt(column_of(stats, EXPERTS) / D + NORM_EPS)
    affinity = 1.0 / (1.0 + jnp.exp(-(stats * inverse)))
    lane_f = lane.astype(F32)
    chosen0 = jnp.sum(jnp.where(lane_f == route0, affinity, 0.0), axis=1, keepdims=True)
    chosen1 = jnp.sum(jnp.where(lane_f == route1, affinity, 0.0), axis=1, keepdims=True)
    scale = ROUTE_SCALE / (chosen0 + chosen1)
    MS[...] = jnp.where(
        lane == 0, chosen0 * scale, jnp.where(lane == 1, chosen1 * scale, inverse)
    )
    scale_half = lax.rem(k, 2)

    def scale_copy(y, t):
        target = jnp.where(k < 4, along(-t), along(1 + t))
        return remote(
            MS.at[pl.ds(pl.multiple_of(scale_half * 32, 32), 32), :], MR.at[t], ms_s.at[y, t],
            ms_r.at[t], (y * 8 + target, e),
        )

    def scale_stays(y, t):
        return (k < 4) & (t == 0) & (y == yl)

    @pl.when(yl == scale_row)
    def _():
        for t in range(4):
            for y in range(2):

                @pl.when(jnp.logical_not(scale_stays(y, t)))
                def _():
                    scale_copy(y, t).start()

                @pl.when(scale_stays(y, t))
                def _():
                    MR[t] = MS[pl.ds(pl.multiple_of(scale_half * 32, 32), 32), :]

    row_copy(c_y, "y").wait_recv()

    row_copy(c_y, "up").start()
    row_copy(c_y, "down").start()

    def arrive(zz, way, go_on):
        own, other = yl * 8 + zz, (1 - yl) * 8 + zz
        row_copy(own, way).wait_recv()

        @pl.when(go_on)
        def _():
            row_copy(own, way).start()

        row_copy(other, way).wait_recv()

        @pl.when(go_on)
        def _():
            row_copy(other, way).start()

    def chunk(t):
        return along(t), along(-1 - t)

    def places(t):
        za, zb = chunk(t)
        return [(0, za), (1, za), (0, zb), (1, zb)]

    def part(kk):
        return pl.ds(pl.multiple_of(kk * 32, 32), 32)

    def half_copy(t, d):
        kk = lax.rem(k + d, 8)
        return remote(
            GS.at[t, :, part(kk), :], GR.at[t, k], g_s.at[t, d], g_r.at[t, k], (c, 2 * kk + s)
        )

    def first_layers(t):
        for i, (y, zz) in enumerate(places(t)):
            XC[t, i * 64 : (i + 1) * 64, :] = X[rows_of(y * 8 + zz), :]
        acc0[...] = jnp.zeros(acc0.shape, F32)
        acc1[...] = jnp.zeros(acc1.shape, F32)
        routed_here = XC[t, :, SL:1024].astype(F32)
        r0, r1 = column_of(routed_here, 0), column_of(routed_here, 1)

        def one_expert(expert, carry):
            product = dot(XC[t, :, 0:SL], W[expert])
            number = expert.astype(F32)
            acc0[...] += jnp.where(r0 == number, product, 0.0)
            acc1[...] += jnp.where(r1 == number, product, 0.0)
            return carry

        lax.fori_loop(0, EXPERTS, one_expert, 0)
        GS[t, 0] = acc0[...].astype(BF)
        GS[t, 1] = acc1[...].astype(BF)
        for d in range(1, 8):
            half_copy(t, d).start()
        GR[t, k] = GS[t, :, part(k), :]

    def act_copy(t, d):
        kk = lax.rem(k + d, 8)
        block = A.at[t, :, part(k), :]
        return remote(block, block, a_s.at[t, d], a_r.at[t, k], (c, 2 * kk + s))

    def activate(t):
        for d in range(1, 8):
            kk = lax.rem(k + d, 8)
            remote(GR.at[t, k], GR.at[t, kk], g_s.at[t, 0], g_r.at[t, kk], (c, e)).wait_recv()
        @pl.when(scale_source(t) != c)
        def _():
            remote(MR.at[t], MR.at[t], ms_s.at[0, 0], ms_r.at[t], (c, e)).wait_recv()

        here = MR[t]
        inverse_here = column_of(here, 2)
        for r in range(2):
            both = GR[t, 0, r].astype(F32)
            for kk in range(1, 8):
                both = both + GR[t, kk, r].astype(F32)
            both = both * inverse_here
            weight = column_of(here, r)
            gate, up = both[:, 0:128], both[:, 128:256]
            A[t, r, part(k), :] = (gate / (1.0 + jnp.exp(-gate)) * up * weight).astype(BF)
        for d in range(1, 8):
            act_copy(t, d).start()

    def partner_copy(y, zz):
        return remote(DP.at[zz, y], YB.at[zz], yb_s.at[zz], yb_r.at[zz], (c_y, e))

    def second_layer(t):
        for d in range(1, 8):
            kk = lax.rem(k + d, 8)
            block = A.at[t, :, part(kk), :]
            remote(block, block, a_s.at[t, 0], a_r.at[t, kk], (c, e)).wait_recv()
        routed_here = XC[t, :, SL:1024].astype(F32)
        r0, r1 = column_of(routed_here, 0), column_of(routed_here, 1)
        a0, a1 = A[t, 0].astype(F32), A[t, 1].astype(F32)
        for expert in range(EXPERTS):
            picked = jnp.where(r0 == float(expert), a0, 0.0) + jnp.where(
                r1 == float(expert), a1, 0.0
            )
            AC[:, expert * 128 : (expert + 1) * 128] = picked.astype(BF)
        out = dot(AC[...], WD[...])
        for i, (y, zz) in enumerate(places(t)):
            DP[zz, y] = out[i * 64 : (i + 1) * 64, :].astype(BF)

        @pl.when(s == 1)
        def _():
            for zz in chunk(t):
                partner_copy(1 - yl, zz).start()

    def down_share(kk, core):
        block = WD.at[down_rows(2 * kk + core), :]
        return remote(block, block, df_s.at[kk], df_r.at[kk], (c, sib))

    arrive(near[1], "up", True)
    share_weight(7)

    def layer_step(t, carry):
        @pl.when(t < 3)
        def _():
            arrive(along(t + 1), "down", t < 2)
            arrive(along(-2 - t), "up", t < 2)

        @pl.when(t == 0)
        def _():
            for kk in range(8):
                weight_share(kk, 1 - s).wait_recv()
            for d in range(1, 8):
                down_weight(d).start()

        @pl.when(t < 4)
        def _():
            first_layers(t)

        @pl.when((t > 0) & (t < 5))
        def _():
            activate(t - 1)

        @pl.when(t == 3)
        def _():
            own_down.wait()
            down_share(k, s).start()
            for d in range(1, 8):
                block = down_rows_of(d)
                kk = lax.rem(k + d, 8)
                remote(block, block, d_s.at[0], d_r.at[kk], (c, e)).wait_recv()
                down_share(kk, s).start()

        @pl.when(t == 4)
        def _():
            for kk in range(8):
                down_share(kk, 1 - s).wait_recv()

        @pl.when(t > 3)
        def _():
            second_layer(t - 4)

        return carry

    lax.fori_loop(0, 8, layer_step, 0)

    routed_all = X[:, SL:1024].astype(F32)
    lane_all = iota(routed_all.shape, 1).astype(F32)
    named = jnp.where(lane_all == column_of(routed_all, 0), 1.0, 0.0) + jnp.where(
        lane_all == column_of(routed_all, 1), 1.0, 0.0
    )
    CS[...] = jnp.broadcast_to(jnp.sum(named, axis=0, keepdims=True), CS.shape)
    count_copy = remote(CS, CR, c_s.at[0], c_r.at[0], (c, sib))
    count_copy.start()

    def joins(y):
        return (s == 0) | (y == yl)

    def complete(zz):
        @pl.when(s == 1)
        def _():
            partner_copy(yl, zz).wait_recv()
            DP[zz, yl] = (DP[zz, yl].astype(F32) + YB[zz].astype(F32)).astype(BF)

    def up_copy(source, step, y):
        return remote(source, RP.at[step, y], p_s.at[step, y], p_r.at[step, y], (c_up, e))

    def down_copy(source, step, y):
        return remote(source, RM.at[step, y], m_s.at[step, y], m_r.at[step, y], (c_down, e))

    ups = [along(4 - t) for t in range(5)]
    downs = [along(t - 3) for t in range(4)]
    complete(ups[0])
    complete(downs[0])
    for y in range(2):

        @pl.when(joins(y))
        def _():
            up_copy(DP.at[ups[0], y], 0, y).start()
            down_copy(DP.at[downs[0], y], 0, y).start()

    for t in range(1, 4):
        complete(ups[t])
        complete(downs[t])
        for y in range(2):

            @pl.when(joins(y))
            def _():
                up_copy(SP.at[0, y], t - 1, y).wait_recv()
                SP[t - 1, y] = (
                    DP[ups[t], y].astype(F32) + RP[t - 1, y].astype(F32)
                ).astype(BF)
                up_copy(SP.at[t - 1, y], t, y).start()
                if t < 3:
                    down_copy(SM.at[0, y], t - 1, y).wait_recv()
                    SM[t - 1, y] = (
                        DP[downs[t], y].astype(F32) + RM[t - 1, y].astype(F32)
                    ).astype(BF)
                    down_copy(SM.at[t - 1, y], t, y).start()

    def final(y):
        down_copy(SM.at[0, 0], 2, y).wait_recv()
        up_copy(SP.at[0, 0], 3, y).wait_recv()
        return DP[z, y].astype(F32) + RP[3, y].astype(F32) + RM[2, y].astype(F32)

    y_copy = remote(YS, YR, y_s.at[0], y_r.at[0], (c_y, e))

    @pl.when(s == 0)
    def _():
        YS[...] = final(1 - yl).astype(BF)
        y_copy.start()

    OS[...] = final(yl) + residual

    @pl.when(s == 0)
    def _():
        y_copy.wait_recv()
        OS[...] += YR[...].astype(F32)

    def owner_copy(j):
        return remote(
            OS.at[pl.ds(j * 8, 8), :], OR.at[k], o_s.at[j], o_r.at[k], (c, 8 * s + j)
        )

    for j in range(8):

        @pl.when(8 * s + j != e)
        def _():
            owner_copy(j).start()

        @pl.when(8 * s + j == e)
        def _():
            OR[k] = OS[pl.ds(j * 8, 8), :]

    count_copy.wait_recv()
    counts = (CS[...] + CR[...])[0:1, 0:EXPERTS]
    load_out[...] = LOAD_DECAY * ema[...] + (1.0 - LOAD_DECAY) * counts / 256.0

    for zz in range(8):
        sib_copy(zz).wait_send()
        weight_share(zz, s).wait_send()
        down_share(zz, s).wait_send()

        @pl.when(2 * zz + e_half != e)
        def _():
            hidden_copy(zz).wait_send()

        @pl.when(s == 1)
        def _():
            partner_copy(1 - yl, zz).wait_send()

    for d in range(1, 8):
        proj_copy(d).wait_send()
        down_weight(d).wait_send()
        stat_copy(d).wait_send()
        for which in range(2):
            weight_copy(d, which).wait_send()
        for t in range(4):
            chip_copy(t, d).wait_send()
            half_copy(t, d).wait_send()
            act_copy(t, d).wait_send()
    for zz in range(8):
        proj_share(yl, zz).wait_send()

    @pl.when(jnp.logical_not(turn_self))
    def _():
        turn_copy(0).wait_send()

    for t in range(1, 4):
        turn_copy(t).wait_send()
    for half in range(2):
        for t in range(4):
            ho_copy(below[t], half, True).wait_send()
        for t in range(3):
            ho_copy(above[t], half, False).wait_send()

    both_rows = yl == 1
    for t in range(8):
        zz = lax.rem(z + t, 8)
        if t > 0:
            kv_share(yl, zz, s).wait_send()

        @pl.when(yl == 1)
        def _():
            kv_share(0, zz, s).wait_send()

        @pl.when((yl == 0) & (zz == z))
        def _():
            kv_copy(0, zz, "y").wait_send()

        @pl.when(zz == z)
        def _():
            row_copy(yl * 8 + zz, "y").wait_send()

    for t in range(4):
        kv_copy(yl, near[t], "up").wait_send()
        row_copy(yl * 8 + near[t], "up").wait_send()

        @pl.when(both_rows)
        def _():
            kv_copy(0, near[t], "up").wait_send()

        row_copy((1 - yl) * 8 + near[t], "up").wait_send()

    for t in range(3):
        kv_copy(yl, far[t], "down").wait_send()
        row_copy(yl * 8 + far[t], "down").wait_send()

        @pl.when(both_rows)
        def _():
            kv_copy(0, far[t], "down").wait_send()

        row_copy((1 - yl) * 8 + far[t], "down").wait_send()

    for y in range(2):

        @pl.when(joins(y))
        def _():
            up_copy(DP.at[ups[0], y], 0, y).wait_send()
            down_copy(DP.at[downs[0], y], 0, y).wait_send()
            for t in range(1, 4):
                up_copy(SP.at[t - 1, y], t, y).wait_send()
                if t < 3:
                    down_copy(SM.at[t - 1, y], t, y).wait_send()

    @pl.when(s == 0)
    def _():
        y_copy.wait_send()

    count_copy.wait_send()

    @pl.when(yl == scale_row)
    def _():
        for t in range(4):
            for y in range(2):

                @pl.when(jnp.logical_not(scale_stays(y, t)))
                def _():
                    scale_copy(y, t).wait_send()

    for j in range(8):

        @pl.when(8 * s + j != e)
        def _():
            owner_copy(j).wait_send()

    for kk in range(8):

        @pl.when(2 * kk + e_half != e)
        def _():
            remote(
                OS.at[pl.ds(0, 8), :], OR.at[kk], o_s.at[0], o_r.at[kk], (c, e)
            ).wait_recv()

        layer_out[:, kk * SL : (kk + 1) * SL] = OR[kk].astype(BF)


def in_vmem(count):
    return [pl.BlockSpec(memory_space=pltpu.VMEM)] * count


def anywhere(count):
    return [pl.BlockSpec(memory_space=pl.ANY)] * count


def dma(*shape):
    return pltpu.SemaphoreType.DMA(shape)


def shaped(shape, dtype):
    return jax.ShapeDtypeStruct(shape, dtype)


def params(number):
    return pltpu.CompilerParams(
        collective_id=number, has_side_effects=True, vmem_limit_bytes=VMEM_LIMIT
    )


def body(
    hidden, q_nope, q_rope, kv_latent, k_rope, key_up, value_up, out_proj, ffn_gain, router,
    w_gate, w_up, w_down, routes, load_ema,
):
    v = pltpu.VMEM
    layer_out, new_load = pl.pallas_call(
        layer_kernel,
        out_shape=(shaped((8, D), BF), shaped((1, EXPERTS), F32)),
        in_specs=in_vmem(10) + anywhere(5),
        out_specs=tuple(in_vmem(2)),
        scratch_shapes=[
            v((2048, 640), BF), v((512, 640), BF), v((512, 1), F32), v((512, 1), F32),
            v((512, 512), F32), v((1024, 512), BF), v((512, SL), BF), v((8, 128, SL), BF),
            v((8, 64, SL), BF), v((4, 128, SL), BF), v((4, 8, 16, SL), BF), v((4, 16, SL), BF),
            v((64, SL), BF), v((8, 8, 1024), F32), v((8, 8, 1024), F32),
            v((1024, 1024), BF), v((16, SL, 256), BF), v((128, SL), BF), v((8, 64, META), F32),
            v((4, 256, 1024), BF), v((256, 256), F32), v((256, 256), F32),
            v((4, 2, 256, 256), BF), v((4, 8, 2, 32, 256), BF), v((4, 2, 256, 128), BF),
            v((2048, SL), BF), v((256, 2048), BF), v((8, 2, 64, SL), BF), v((8, 64, SL), BF),
            v((4, 2, 64, SL), BF), v((3, 2, 64, SL), BF), v((3, 2, 64, SL), BF),
            v((2, 2, 64, SL), BF), v((64, SL), BF), v((64, SL), BF), v((64, SL), F32),
            v((8, 8, SL), F32), v((8, 128), F32), v((8, 128), F32), v((64, META), F32),
            v((4, 32, META), F32),
            dma(5), dma(16), dma(16), dma(16), dma(16), dma(16), dma(16), dma(8), dma(8),
            dma(8), dma(8), dma(8), dma(8),
            dma(8, 2), dma(8, 2), dma(8), dma(8), dma(8, 2), dma(8, 2), dma(8, 2), dma(8), dma(8),
            dma(4, 8), dma(4, 8), dma(4), dma(4),
            dma(8), dma(8), dma(8), dma(8), dma(8), dma(8), dma(16), dma(16), dma(16), dma(16),
            dma(4, 8), dma(4, 8), dma(4, 8), dma(4, 8),
            dma(8), dma(8), dma(4, 2), dma(4, 2), dma(3, 2), dma(3, 2), dma(1), dma(1), dma(8),
            dma(8), dma(1), dma(1), dma(2, 4), dma(4),
        ],
        compiler_params=params(0),
        name="layer",
    )(
        q_nope, q_rope, kv_latent, k_rope.T, key_up, value_up, hidden, routes.T,
        ffn_gain.reshape(8, 1, SL), load_ema.reshape(1, EXPERTS), out_proj, router.T, w_gate, w_up, w_down,
    )
    return layer_out, new_load.reshape(EXPERTS)


def solution(mesh):
    placed = (
        P(("ctx", "ep"), None),
        P("ctx", "ep"),
        P("ctx", "ep"),
        P("ctx", None),
        P("ctx", None),
        P(None, "ep"),
        P(None, "ep"),
        P(("ep", "ctx"), None),
        P(),
        P(),
        P("ep", None, "ctx"),
        P("ep", None, "ctx"),
        P("ep", "ctx", None),
        P(("ctx", "ep"), None),
        P(),
    )
    return jax.shard_map(
        body, mesh=mesh, in_specs=placed, out_specs=(P(("ctx", "ep"), None), P()), check_vma=False
    )
```
